256 devices in a mesh: segment: 4 (over x_lo, core), rows: 64 (over y, x_hi, z).
Axes of the slice: x: 4 (x_hi: 2, x_lo: 2; x = x_hi * 2 + x_lo), y: 4, z: 8, core: 2. Of those that a mesh axis runs over, the one named last changes fastest.
Arguments:
- features: bfloat16 [2, 4, 64, 16, 384], P(None, None, 'rows'), may hold values from -6 to 6
- cache_zero: bfloat16 [2, 2, 64, 16, 384], P(None, None, 'rows'), may hold values from -6 to 6
- cache_one: bfloat16 [2, 2, 128, 32, 384], P(None, None, 'rows'), may hold values from -6 to 6
- cache_two: bfloat16 [2, 2, 256, 64, 384], P(None, None, 'rows'), may hold values from -6 to 6
- cache_three: bfloat16 [2, 2, 512, 128, 192], P(None, None, 'rows'), may hold values from -6 to 6
- gain_zero: float32 [384], replicated, may hold values from 0.4 to 1.6
- gain_one: float32 [384], replicated, may hold values from 0.4 to 1.6
- gain_two: float32 [384], replicated, may hold values from 0.4 to 1.6
- gain_three: float32 [192], replicated, may hold values from 0.4 to 1.6
- weight_zero: bfloat16 [1152, 3, 3, 384], P('rows'), may hold values from -0.0625 to 0.0625
- weight_one: bfloat16 [1152, 3, 3, 384], P('rows'), may hold values from -0.0625 to 0.0625
- weight_two: bfloat16 [1152, 3, 3, 192], P('rows'), may hold values from -0.0625 to 0.0625
- weight_three: bfloat16 [576, 3, 3, 96], P('rows'), may hold values from -0.078125 to 0.078125
- proj_two: bfloat16 [384, 192], replicated, may hold values from -0.3125 to 0.3125
- proj_three: bfloat16 [192, 96], replicated, may hold values from -0.4375 to 0.4375
Outputs:
- decoded: bfloat16 [2, 4, 96, 512, 128], P(None, 'segment', None, 'rows')
The draws below stay inside these ranges and needn't reach their ends.
All inputs are finite; a program needn't handle non-finite values.
Results may differ from the reference program's by a relative error of at most 0.0065.
Values may be sent and summed in bfloat16 or wider, within the bound.
No kernel may reach another device: no remote copies, remote signals or barrier semaphores. Data moves between devices by JAX's collectives and lax.ppermute only.
A program may use at most 128 MiB of HBM per device.

```python
import jax
import jax.numpy as jnp
from jax import lax

WIDE = 384
MID = 192
NARROW = 96
VIDEOS = 2
FRAMES = 4
COLS0 = 16
HEIGHT0 = 64
HEIGHT1 = 128
HEIGHT2 = 256
HEIGHT3 = 512
WIDTH1 = 32
WIDTH2 = 64
WIDTH3 = 128


def block_levels(own_key, extent, shards, low, top_value):
    level = 1.0
    for axis_at, blocks in shards:
        draws = jax.random.uniform(jax.random.fold_in(jax.random.fold_in(own_key, 6), axis_at), (blocks,), jnp.float32, low / len(shards), top_value / len(shards))
        level = level * jnp.repeat(jnp.exp(draws), extent[axis_at] // blocks).reshape((-1,) + (1,) * (len(extent) - 1 - axis_at))
    return level


def gaussian(key, shape, spread, bound, split=(), held_as=jnp.bfloat16):
    values = jax.random.normal(key, shape, jnp.float32) * spread
    if len(split) > 0:
        values = block_levels(key, shape, split, -0.22, 0.18) * values
    return jnp.clip(values, min=-bound, max=bound).astype(held_as)


def setup_inputs(seed: int = 0) -> dict:
    streams_of = jax.random.split(jax.random.key(seed), 16)
    features = gaussian(streams_of[0], (VIDEOS, FRAMES, HEIGHT0, COLS0, WIDE), 1.0, 6.0, ((2, 64),))
    cache_zero = gaussian(streams_of[1], (VIDEOS, 2, HEIGHT0, COLS0, WIDE), 1.0, 6.0, ((2, 64),))
    cache_one = gaussian(streams_of[2], (VIDEOS, 2, HEIGHT1, WIDTH1, WIDE), 1.0, 6.0, ((2, 64),))
    cache_two = gaussian(streams_of[3], (VIDEOS, 2, HEIGHT2, WIDTH2, WIDE), 1.0, 6.0, ((2, 64),))
    cache_three = gaussian(streams_of[4], (VIDEOS, 2, HEIGHT3, WIDTH3, MID), 1.0, 6.0, ((2, 64),))
    gain_zero = jnp.clip(1.0 + 0.12 * jax.random.normal(streams_of[5], (WIDE,), jnp.float32), 0.4, 1.6)
    gain_one = jnp.clip(1.0 + 0.12 * jax.random.normal(streams_of[6], (WIDE,), jnp.float32), 0.4, 1.6)
    gain_two = jnp.clip(1.0 + 0.12 * jax.random.normal(streams_of[7], (WIDE,), jnp.float32), 0.4, 1.6)
    gain_three = jnp.clip(1.0 + 0.12 * jax.random.normal(streams_of[8], (MID,), jnp.float32), 0.4, 1.6)
    weight_zero = gaussian(streams_of[9], (3 * WIDE, 3, 3, WIDE), (27 * WIDE) ** -0.5, 0.0625, ((0, 64),))
    weight_one = gaussian(streams_of[10], (3 * WIDE, 3, 3, WIDE), (27 * WIDE) ** -0.5, 0.0625, ((0, 64),))
    weight_two = gaussian(streams_of[11], (3 * WIDE, 3, 3, MID), (27 * WIDE) ** -0.5, 0.0625, ((0, 64),))
    weight_three = gaussian(streams_of[12], (3 * MID, 3, 3, NARROW), (27 * MID) ** -0.5, 0.078125, ((0, 64),))
    proj_two = gaussian(streams_of[13], (WIDE, MID), WIDE ** -0.5, 0.3125)
    proj_three = gaussian(streams_of[14], (MID, NARROW), MID ** -0.5, 0.4375)
    return {"features": features, "cache_zero": cache_zero, "cache_one": cache_one, "cache_two": cache_two, "cache_three": cache_three, "gain_zero": gain_zero, "gain_one": gain_one, "gain_two": gain_two, "gain_three": gain_three, "weight_zero": weight_zero, "weight_one": weight_one, "weight_two": weight_two, "weight_three": weight_three, "proj_two": proj_two, "proj_three": proj_three}


EPSILON = 1e-06

def activate(values, gain_vec):
    widened = values.astype(jnp.float32)
    scaled = widened * lax.rsqrt(lax.optimization_barrier(jnp.mean(widened * widened, axis=-1, keepdims=True)) + EPSILON)
    return jax.nn.silu(scaled * gain_vec.astype(jnp.float32)).astype(jnp.bfloat16)

def enlarge(values):
    return jnp.repeat(jnp.repeat(values, 2, axis=0), 2, axis=1)

def convolve(padded, weight, channels_first):
    frames_in, rows_pad, columns, channels = padded.shape
    height = rows_pad - 2
    wide_pad = jnp.pad(padded, ((0, 0), (0, 0), (1, 1), (0, 0)))
    stacked = jnp.concatenate([wide_pad[:, :, 0:columns], wide_pad[:, :, 1:columns + 1], wide_pad[:, :, 2:columns + 2]], axis=-1)
    summed = None
    for frame_tap in range(3):
        for row_tap in range(3):
            row_block = stacked[frame_tap, row_tap:row_tap + height].reshape(height * columns, 3 * channels)
            if channels_first:
                partial_sum = lax.dot_general(weight[frame_tap, row_tap], row_block, (((0,), (1,)), ((), ())), preferred_element_type=jnp.float32)
            else:
                partial_sum = jnp.dot(row_block, weight[frame_tap, row_tap], preferred_element_type=jnp.float32)
            summed = partial_sum if summed is None else summed + partial_sum
    return summed

def shortcut(segment_in, projection, level):
    flattened = segment_in.reshape(-1, segment_in.shape[-1])
    if level < 2:
        return flattened.astype(jnp.float32)
    if level == 2:
        return jnp.dot(flattened, projection, preferred_element_type=jnp.float32)
    return lax.dot_general(projection, flattened, (((0,), (1,)), ((), ())), preferred_element_type=jnp.float32)

def reference(features, cache_zero, cache_one, cache_two, cache_three, gain_zero, gain_one, gain_two, gain_three, weight_zero, weight_one, weight_two, weight_three, proj_two, proj_three):
    caches = (cache_zero, cache_one, cache_two, cache_three)
    gains = (gain_zero, gain_one, gain_two, gain_three)
    weights = tuple((weight_arr.transpose(1, 2, 0, 3) for weight_arr in (weight_zero, weight_one, weight_two, weight_three)))
    projections = (None, None, proj_two, proj_three)
    videos, frames = (features.shape[0], features.shape[1])
    results = []
    for video_id in range(videos):
        histories = [caches[level][video_id] for level in range(4)]
        outputs = []
        for frame_id in range(frames):
            segment_in = features[video_id, frame_id]
            for level in range(4):
                height, columns = (segment_in.shape[0], segment_in.shape[1])
                newest = activate(segment_in, gains[level])
                window = jnp.concatenate([histories[level], newest[None]], axis=0)
                histories[level] = window[1:]
                padded = jnp.pad(window, ((0, 0), (1, 1), (0, 0), (0, 0)))
                summed = convolve(padded, weights[level], level == 3) + shortcut(segment_in, projections[level], level)
                outcome = summed.astype(jnp.bfloat16)
                out_width = weights[level].shape[-1]
                if level < 3:
                    segment_in = enlarge(outcome.reshape(height, columns, out_width))
                else:
                    outputs.append(outcome.reshape(out_width, height, columns))
        results.append(jnp.stack(outputs))
    return jnp.stack(results)
```

```python
import functools

import jax
import jax.numpy as jnp
from jax import lax
from jax.experimental import pallas as pl
from jax.experimental.pallas import tpu as pltpu
from jax.sharding import Mesh
from jax.sharding import PartitionSpec as P

EPSILON = 1e-06
ROWS = ("y", "xhi", "z")
SEG = ("xlo", "core")
ALL = SEG + ROWS
BF16 = jnp.bfloat16
F32 = jnp.float32


def activate(values, gain_vec):
    widened = values.astype(F32)
    scaled = widened * lax.rsqrt(jnp.mean(widened * widened, axis=-1, keepdims=True) + EPSILON)
    return jax.nn.silu(scaled * gain_vec).astype(BF16)


def permute_rows(x, by, segments=(0, 1, 2, 3)):
    pairs = [(s * 64 + r, s * 64 + r + by) for s in segments for r in range(64) if 0 <= r + by < 64]
    return lax.ppermute(x, ALL, pairs)


def both_videos(own):
    other = lax.ppermute(own, "core", [(0, 1), (1, 0)])
    first = lax.axis_index("core") == 0
    return jnp.stack([jnp.where(first, own, other), jnp.where(first, other, own)])


def with_halo(x, width, segments=(0, 1, 2, 3)):
    rows = x.shape[2]
    half = lax.dynamic_index_in_dim(x, lax.axis_index("core"), 0, keepdims=False)
    reach = -(-width // rows)
    above, below = [], []
    for by in range(reach, 0, -1):
        take = width - (reach - 1) * rows if by == reach else rows
        above.append(permute_rows(half[:, rows - take :], by, segments))
    for by in range(1, reach + 1):
        take = width - (reach - 1) * rows if by == reach else rows
        below.append(permute_rows(half[:, :take], -by, segments))
    rim = both_videos(jnp.concatenate(above + below, axis=1))
    return jnp.concatenate([rim[:, :, :width], x, rim[:, :, width:]], axis=2)


def gather_weights(shard):
    k, lanes = shard.shape
    spread = jnp.broadcast_to(shard[None], (16, k, lanes))
    block = lax.all_to_all(spread, ("xhi", "z"), 0, 0, tiled=True).reshape(16 * k, lanes)
    up = [(i, (i + 1) % 4) for i in range(4)]
    down = [(j, i) for i, j in up]
    at = lax.axis_index("y")
    half = 8 * k
    from_below = lax.ppermute(block, "y", up)
    from_above = lax.ppermute(block, "y", down)
    far_top = lax.ppermute(from_below[:half], "y", up)
    far_bottom = lax.ppermute(from_above[half:], "y", down)
    whole = jnp.zeros((4, 16 * k, lanes), shard.dtype)
    for piece, off, row in (
        (block, 0, 0),
        (from_below, 3, 0),
        (from_above, 1, 0),
        (far_top, 2, 0),
        (far_bottom, 2, half),
    ):
        whole = lax.dynamic_update_slice(whole, piece[None], ((at + off) % 4, row, 0))
    return whole.reshape(64 * k, lanes)


def gather_segment(x):
    own = lax.axis_index("xlo") * 2 + lax.axis_index("core")
    whole = jnp.zeros((4,) + x.shape, x.dtype)
    for d in range(4):
        piece = x if d == 0 else lax.ppermute(x, SEG, [(i, (i + d) % 4) for i in range(4)])
        whole = lax.dynamic_update_slice(whole, piece[None], ((own - d) % 4,) + (0,) * x.ndim)
    whole = jnp.moveaxis(whole, 0, -2)
    return whole.reshape(x.shape[:-1] + (4 * x.shape[-1],))


def spreader(columns, source, doubled, taps=(0, 1, 2)):
    parts = []
    for tap in taps:
        at = lax.broadcasted_iota(jnp.int32, (columns, source), 0) + (tap - 1)
        held = lax.broadcasted_iota(jnp.int32, (columns, source), 1)
        low = 2 * held if doubled else held
        high = low + 1 if doubled else low
        parts.append(jnp.where((at >= low) & (at <= high), 1.0, 0.0).astype(BF16))
    return parts[0] if len(parts) == 1 else jnp.concatenate(parts, axis=0)


def level_kernel(dims, edge_ref, u_ref, cache_ref, side_ref, weight_ref, *rest):
    columns, doubled, out_rows, project = dims
    if project:
        proj_ref, out_ref, stacked, product, shortcut = rest
    else:
        out_ref, stacked, product, shortcut = rest
    channels = u_ref.shape[4]
    n = out_ref.shape[4]
    rows_u, rows_c, rows_s = u_ref.shape[2], cache_ref.shape[2], side_ref.shape[2]
    source = u_ref.shape[3]
    fine = spreader(columns, columns, False)
    coarse = spreader(columns, source, doubled)
    middle = spreader(columns, source, doubled, (1,))

    def put(row_at, matrix, values):
        spread = jnp.dot(matrix, values, preferred_element_type=F32).astype(BF16)
        for tap in range(3):
            stacked[pl.ds(row_at, columns), tap * channels : (tap + 1) * channels] = spread[
                tap * columns : (tap + 1) * columns
            ]

    cache_size, u_size = rows_c * columns, rows_u * columns
    video_size = 2 * cache_size + 4 * u_size

    def fill(video, carry):
        for frame in range(2):
            for row in range(rows_c):
                at = video * video_size + frame * cache_size + row * columns
                put(pl.multiple_of(at, columns), fine, cache_ref[video, frame, row])
        for frame in range(4):
            for row in range(rows_u):
                at = video * video_size + 2 * cache_size + frame * u_size + row * columns
                put(pl.multiple_of(at, columns), coarse, u_ref[video, frame, row])
            for row in range(rows_s):
                own = jnp.dot(middle, side_ref[video, frame, row], preferred_element_type=F32)
                if project:
                    own = jnp.dot(own.astype(BF16), proj_ref[...], preferred_element_type=F32)
                at = ((video * 4 + frame) * rows_s + row) * columns
                shortcut[pl.ds(pl.multiple_of(at, columns), columns), :] = own
        return carry

    lax.fori_loop(0, 2, fill, 0)

    total = 2 * video_size
    chunk = next(c for c in (512, 384, 256, 320, 480, 192, 128, 96, 64) if total % c == 0)

    def multiply(step, carry):
        at = pl.multiple_of(step * chunk, chunk)
        product[pl.ds(at, chunk), :] = jnp.dot(
            stacked[pl.ds(at, chunk), :], weight_ref[...], preferred_element_type=F32
        )
        return carry

    lax.fori_loop(0, total // chunk, multiply, 0)

    first, last = edge_ref[0], edge_ref[1]

    def add_up(video, carry):
        for frame in range(4):
            for row in range(out_rows):
                summed = None
                for frame_tap in range(3):
                    held = frame + frame_tap
                    for row_tap in range(3):
                        wanted = row + row_tap
                        if held < 2:
                            at = held * cache_size + wanted * columns
                        else:
                            at = 2 * cache_size + (held - 2) * u_size
                            at = at + (wanted // 2 if doubled else wanted) * columns
                        at = pl.multiple_of(video * video_size + at, columns)
                        lane = (3 * frame_tap + row_tap) * n
                        part = product[pl.ds(at, columns), lane : lane + n]
                        summed = part if summed is None else summed + part
                held_row = (row + 1) // 2 if doubled else row
                at = ((video * 4 + frame) * rows_s + held_row) * columns
                summed = summed + shortcut[pl.ds(pl.multiple_of(at, columns), columns), :]
                if row == 0:
                    summed = jnp.where(first == 1, 0.0, summed)
                if row == out_rows - 1:
                    summed = jnp.where(last == 1, 0.0, summed)
                out_ref[video, frame, row] = summed.astype(BF16)
        return carry

    lax.fori_loop(0, 2, add_up, 0)


def run_level(edges, u, cache, side, weight, out_rows, project=None):
    columns = cache.shape[3]
    channels = cache.shape[4]
    doubled = u.shape[3] != columns
    n = weight.shape[1] // 9
    total = 2 * (2 * cache.shape[2] + 4 * u.shape[2]) * columns
    vmem = pl.BlockSpec(memory_space=pltpu.VMEM)
    operands = [edges, u, cache, side, weight] + ([] if project is None else [project])
    flops = 2 * total * 3 * channels * 9 * n
    return pl.pallas_call(
        functools.partial(level_kernel, (columns, doubled, out_rows, project is not None)),
        out_shape=jax.ShapeDtypeStruct((2, 4, out_rows, columns, n), BF16),
        in_specs=[pl.BlockSpec(memory_space=pltpu.SMEM)] + [vmem] * (len(operands) - 1),
        out_specs=vmem,
        scratch_shapes=[
            pltpu.VMEM((total, 3 * channels), BF16),
            pltpu.VMEM((total, 9 * n), F32),
            pltpu.VMEM((8 * side.shape[2] * columns, n), F32),
        ],
        compiler_params=pltpu.CompilerParams(vmem_limit_bytes=44 * 2**20),
        cost_estimate=pl.CostEstimate(flops=4 * flops, bytes_accessed=4 * 2**20, transcendentals=0),
    )(*operands)


def last_kernel(place_ref, u_ref, cache_ref, side_ref, weight_ref, proj_ref, out_ref, stacked, summed):
    columns, channels, n = 128, 192, 96
    place = place_ref[0]
    fine = spreader(columns, columns, False)
    coarse = spreader(columns, 64, True)
    middle = spreader(columns, 64, True, (1,))

    def one_video(video, carry):
        def put(frame, row, spread):
            for tap in range(3):
                stacked[tap, frame, row * columns : (row + 1) * columns, :] = spread[
                    tap * columns : (tap + 1) * columns
                ]

        for frame in range(3):
            from_cache = place + frame < 2

            @pl.when(from_cache)
            def _():
                for row in range(10):
                    values = cache_ref[video, jnp.minimum(place + frame, 1), row]
                    put(frame, row, jnp.dot(fine, values, preferred_element_type=F32).astype(BF16))

            @pl.when(jnp.logical_not(from_cache))
            def _():
                for row in range(6):
                    spread = jnp.dot(coarse, u_ref[video, frame, row], preferred_element_type=F32)
                    spread = spread.astype(BF16)
                    for copy in (2 * row - 1, 2 * row):
                        if 0 <= copy < 10:
                            put(frame, copy, spread)

        for row in range(8):
            if row % 2 == 0:
                own = jnp.dot(middle, side_ref[video, 1 + row // 2], preferred_element_type=F32)
                own = jnp.dot(own.astype(BF16), proj_ref[...], preferred_element_type=F32)
            summed[row * columns : (row + 1) * columns, :] = own

        for frame_tap in range(3):
            for row_tap in range(3):
                lane = (3 * frame_tap + row_tap) * n
                part = None
                for tap in range(3):
                    term = jnp.dot(
                        stacked[tap, frame_tap, row_tap * columns : (row_tap + 8) * columns, :],
                        weight_ref[tap * channels : (tap + 1) * channels, lane : lane + n],
                        preferred_element_type=F32,
                    )
                    part = term if part is None else part + term
                summed[...] += part

        for row in range(8):
            out_ref[video, row] = summed[row * columns : (row + 1) * columns, :].T.astype(BF16)
        return carry

    lax.fori_loop(0, 2, one_video, 0)


def run_last(place, u, cache, side, weight, proj):
    vmem = pl.BlockSpec(memory_space=pltpu.VMEM)
    return pl.pallas_call(
        last_kernel,
        out_shape=jax.ShapeDtypeStruct((2, 8, 96, 128), BF16),
        in_specs=[pl.BlockSpec(memory_space=pltpu.SMEM)] + [vmem] * 5,
        out_specs=vmem,
        scratch_shapes=[
            pltpu.VMEM((3, 3, 1280, 192), BF16),
            pltpu.VMEM((1024, 96), F32),
        ],
        compiler_params=pltpu.CompilerParams(vmem_limit_bytes=44 * 2**20),
        cost_estimate=pl.CostEstimate(flops=10**10, bytes_accessed=4 * 2**20, transcendentals=0),
    )(place, u, cache, side, weight, proj)


def shards(
    features,
    cache_zero,
    cache_one,
    cache_two,
    cache_three,
    gain_zero,
    gain_one,
    gain_two,
    gain_three,
    weight_zero,
    weight_one,
    weight_two,
    weight_three,
    proj_two,
    proj_three,
):
    place = lax.axis_index("xlo") * 2 + lax.axis_index("core")
    row_at = lax.axis_index(ROWS)
    edges = jnp.stack([row_at == 0, row_at == 63]).astype(jnp.int32)

    def quarter(x):
        width = x.shape[-1] // 4
        return lax.dynamic_slice_in_dim(x, place * width, width, x.ndim - 1)

    def own_shard(weight, split=True):
        part = quarter(weight) if split else weight
        return part.reshape(part.shape[0], -1)

    w0 = gather_weights(own_shard(weight_zero))
    start = with_halo(jnp.concatenate([cache_zero, features], axis=1), 2)
    w1 = gather_weights(own_shard(weight_one))
    held_one = with_halo(cache_one, 2)
    w2 = gather_weights(own_shard(weight_two))
    held_two = with_halo(cache_two, 2)
    w3 = gather_weights(own_shard(weight_three, False))
    held_three = with_halo(cache_three, 1, (0, 1))

    x0 = start[:, 2:]
    u0 = activate(x0, gain_zero)
    own0 = run_level(edges, u0, start[:, :2], quarter(x0[:, :, 1:4]), w0, 3)
    u1 = activate(gather_segment(own0), gain_one)
    own1 = run_level(edges, u1, held_one, own0, w1, 4)
    x2 = gather_segment(own1)
    u2 = activate(x2, gain_two)
    own2 = run_level(edges, u2, held_two, x2, w2, 6, quarter(proj_two))
    x3 = gather_segment(own2)
    padded = jnp.pad(x3, ((0, 0), (2, 0), (0, 0), (0, 0), (0, 0)))
    x3 = lax.dynamic_slice_in_dim(padded, place, 3, 1)
    u3 = activate(x3, gain_three)
    out = run_last(place[None], u3, held_three, x3[:, 2], w3, proj_three)
    return out.transpose(0, 2, 1, 3)[:, None]


def solution(mesh):
    fine_mesh = Mesh(mesh.devices.reshape(2, 2, 4, 2, 8), ALL)
    slab = P(None, None, ROWS, None, None)
    shard = P(ROWS, None, None, None)
    return jax.shard_map(
        shards,
        mesh=fine_mesh,
        in_specs=(slab,) * 5 + (P(),) * 4 + (shard,) * 4 + (P(),) * 2,
        out_specs=P(None, SEG, None, ROWS, None),
        check_vma=False,
    )
```

```python
import functools

import jax
import jax.numpy as jnp
from jax import lax
from jax.experimental import pallas as pl
from jax.experimental.pallas import tpu as pltpu
from jax.sharding import Mesh
from jax.sharding import PartitionSpec as P

EPSILON = 1e-06
ROWS = ("y", "xhi", "z")
SEG = ("xlo", "core")
ALL = SEG + ROWS
BF16 = jnp.bfloat16
F32 = jnp.float32


def after(x, *others):
    return lax.optimization_barrier((x,) + others)[0]


def fetch_rows(x, by):
    pairs = []
    for segment in range(4):
        step = by if segment % 2 == 0 else -by
        pairs += [(segment * 64 + r + step, segment * 64 + r) for r in range(64) if 0 <= r + step < 64]
    return lax.ppermute(x, ALL, pairs)


def both_sides(own):
    core = lax.axis_index("core")
    other = lax.ppermute(own, "core", [(0, 1), (1, 0)])
    return jnp.where(core == 1, own, other), jnp.where(core == 0, own, other)


def with_first_halo(start):
    flat = start.reshape(-1, start.shape[-1])
    size = flat.shape[0]
    above, below = both_sides(jnp.concatenate([fetch_rows(flat, 1), fetch_rows(flat, 2)], axis=0))
    rows = [above[size:], above[:size], flat, below[:size], below[size:]]
    return jnp.concatenate([x.reshape(start.shape) for x in rows], axis=2)


def with_halos(one, two, three):
    upper = lax.axis_index("core")
    two_rows = lax.dynamic_slice_in_dim(two, upper * (two.shape[2] - 2), 2, 2)
    three_rows = lax.dynamic_slice_in_dim(three, upper * (three.shape[2] - 1), 1, 2)[:, :, 0]
    sides = jnp.concatenate([three_rows[:, 0], three_rows[:, 1]], axis=-1)
    flat = [x.reshape(-1, 384) for x in (one, two_rows, sides)]
    rims = both_sides(fetch_rows(jnp.concatenate(flat, axis=0), 1))
    ones = [rim[:256].reshape(2, 2, 2, 32, 384) for rim in rims]
    twos = [rim[256:768].reshape(2, 2, 2, 64, 384) for rim in rims]
    sides = [rim[768:].reshape(2, 128, 384) for rim in rims]
    threes = [jnp.stack([x[..., :192], x[..., 192:]], axis=1)[:, :, None] for x in sides]
    return (
        jnp.concatenate([ones[0], one, ones[1]], axis=2),
        jnp.concatenate([twos[0], two, twos[1]], axis=2),
        jnp.concatenate([threes[0], three, threes[1]], axis=2),
    )


def with_other_plane(x):
    other = lax.ppermute(x, "xhi", [(0, 1), (1, 0)])
    first = lax.axis_index("xhi") == 0
    return jnp.concatenate([jnp.where(first, x, other), jnp.where(first, other, x)], axis=0)


def ring_z(mine):
    up = [(i, (i + 1) % 8) for i in range(8)]
    down = [(j, i) for i, j in up]
    half = mine.shape[0] // 2
    pieces = [mine]
    rising = falling = mine
    for step in range(1, 5):
        if step == 4:
            rising, falling = rising[:half], falling[half:]
        rising = lax.ppermute(rising, "z", up)
        falling = lax.ppermute(falling, "z", down)
        pieces += [rising, falling]
    return pieces


def share_ring(block, *wait_for):
    up = [(i, (i + 1) % 4) for i in range(4)]
    down = [(j, i) for i, j in up]
    half = block.shape[0] // 2
    sent = after(block, *wait_for) if wait_for else block
    from_below = lax.ppermute(sent, "y", up)
    from_above = lax.ppermute(sent, "y", down)
    far_top = lax.ppermute(from_below[:half], "y", up)
    far_bottom = lax.ppermute(from_above[half:], "y", down)
    return [block, from_below, from_above, far_top, far_bottom]


def share_segment(pieces):
    return [pieces[0]] + [
        lax.ppermute(pieces[d], SEG, [(i, (i + d) % 4) for i in range(4)]) for d in (1, 2, 3)
    ]


VMEM = pl.BlockSpec(memory_space=pltpu.VMEM)
SMEM = pl.BlockSpec(memory_space=pltpu.SMEM)
PARAMS = pltpu.CompilerParams(vmem_limit_bytes=44 * 2**20)


def spreader(columns, source, doubled, taps=(0, 1, 2)):
    parts = []
    for tap in taps:
        at = lax.broadcasted_iota(jnp.int32, (columns, source), 0) + (tap - 1)
        held = lax.broadcasted_iota(jnp.int32, (columns, source), 1)
        low = 2 * held if doubled else held
        high = low + 1 if doubled else low
        parts.append(jnp.where((at >= low) & (at <= high), 1.0, 0.0).astype(BF16))
    return parts[0] if len(parts) == 1 else jnp.concatenate(parts, axis=0)


def placer(width, lanes, offset, low=0, high=None):
    row = lax.broadcasted_iota(jnp.int32, (width, lanes), 0)
    lane = lax.broadcasted_iota(jnp.int32, (width, lanes), 1)
    hit = (lane == row - low + offset) & (row >= low) & (row < (width if high is None else high))
    return jnp.where(hit, 1.0, 0.0)


def normed(x, gain):
    scaled = x * lax.rsqrt(jnp.mean(x * x, axis=-1, keepdims=True) + EPSILON)
    scaled = scaled * gain
    return (scaled / (1.0 + jnp.exp(-scaled))).astype(BF16)


def set_weights(at, pieces, whole, base=0):
    if len(pieces) == 4:
        for piece, off in zip(pieces, (0, 3, 1, 2)):
            low = 0 if off == 2 else base
            whole[lax.rem(at + off, 4)] = piece[low : low + 288]
        return
    whole[...] = pieces[0][:, :, : whole.shape[2]]


def put_taps(stacked, row_at, columns, spread):
    channels = spread.shape[1]
    for tap in range(3):
        stacked[pl.ds(row_at, columns), tap * channels : (tap + 1) * channels] = spread[
            tap * columns : (tap + 1) * columns
        ]


def multiply_all(stacked, whole, product, total):
    chunk = next(c for c in (512, 480, 384, 320, 256, 192, 128, 96, 64) if total % c == 0)

    def multiply(step, carry):
        at = pl.multiple_of(step * chunk, chunk)
        weight = whole[...].reshape(4 * whole.shape[1], whole.shape[2])
        product[pl.ds(at, chunk), :] = jnp.dot(
            stacked[pl.ds(at, chunk), :], weight, preferred_element_type=F32
        )
        return carry

    lax.fori_loop(0, total // chunk, multiply, 0)


def dot(a, b):
    return jnp.dot(a, b, preferred_element_type=F32)


def plane_kernel(scalar_ref, *refs):
    pieces, outs, held = refs[:9], refs[9:11], refs[11]
    at = scalar_ref[4]
    for piece, off in zip(pieces[:7], (0, 7, 1, 6, 2, 5, 3)):
        held[lax.rem(at + off, 8)] = piece[...]
    held[lax.rem(at + 4, 8), :56] = pieces[7][...]
    held[lax.rem(at + 4, 8), 56:] = pieces[8][...]
    for matrix, (out, base) in enumerate(((outs[0], 0), (outs[0], 288), (outs[1], 0))):
        for block in range(16):
            low = 56 * (block // 8) + 18 * matrix
            out[base + 18 * block : base + 18 * (block + 1), :] = held[block % 8, low : low + 18, :]


def run_plane(scalars, pieces):
    return pl.pallas_call(
        plane_kernel,
        out_shape=[jax.ShapeDtypeStruct((576, 864), BF16), jax.ShapeDtypeStruct((288, 864), BF16)],
        in_specs=[SMEM] + [VMEM] * 9,
        out_specs=[VMEM] * 2,
        scratch_shapes=[pltpu.VMEM((8, 112, 864), BF16)],
        compiler_params=PARAMS,
        cost_estimate=pl.CostEstimate(flops=10**8, bytes_accessed=4 * 2**20, transcendentals=0),
    )(scalars, *pieces)


def halves_kernel(whole, out_ref):
    row = lax.broadcasted_iota(jnp.int32, (72, 144), 0)
    lane = lax.broadcasted_iota(jnp.int32, (72, 144), 1)
    for half in range(2):
        pick = jnp.where(lane == 2 * row + half, 1.0, 0.0).astype(BF16)
        for block in range(8):
            rows = whole[block // 2, 144 * (block % 2) : 144 * (block % 2 + 1), 432:]
            out_ref[72 * block : 72 * (block + 1), 432 * half : 432 * (half + 1)] = dot(pick, rows).astype(BF16)


def run_halves(whole):
    return pl.pallas_call(
        halves_kernel,
        out_shape=jax.ShapeDtypeStruct((576, 864), BF16),
        in_specs=[VMEM],
        out_specs=VMEM,
        compiler_params=PARAMS,
        cost_estimate=pl.CostEstimate(flops=10**8, bytes_accessed=4 * 2**20, transcendentals=0),
    )(whole)


def held_kernel(scalar_ref, cache_ref, *refs):
    pieces, (out_ref, whole, stacked, product) = refs[:-4], refs[-4:]
    rows, columns = cache_ref.shape[2], cache_ref.shape[3]
    out_rows, n = out_ref.shape[2], out_ref.shape[4]
    set_weights(scalar_ref[1], pieces, whole, 0 if columns == 16 else 288)
    fine = spreader(columns, columns, False)
    size = rows * columns

    def fill(frame, carry):
        for row in range(rows):
            at = pl.multiple_of(frame * size + row * columns, columns)
            values = cache_ref[frame // 2, lax.rem(frame, 2), row]
            put_taps(stacked, at, columns, dot(fine, values).astype(BF16))
        return carry

    lax.fori_loop(0, 4, fill, 0)
    multiply_all(stacked, whole, product, 4 * size)

    def add_up(video, carry):
        for frame in range(2):
            for row in range(out_rows):
                summed = None
                for frame_tap in range(2 - frame):
                    for row_tap in range(3):
                        at = (frame + frame_tap) * size + (row + row_tap) * columns
                        at = pl.multiple_of(video * 2 * size + at, columns)
                        lane = (3 * frame_tap + row_tap) * n
                        part = product[pl.ds(at, columns), lane : lane + n]
                        summed = part if summed is None else summed + part
                out_ref[video, frame, row] = summed
        return carry

    lax.fori_loop(0, 2, add_up, 0)


def run_held(scalars, cache, pieces, out_rows, n):
    rows, columns, channels = cache.shape[2:]
    total = 4 * rows * columns
    return pl.pallas_call(
        held_kernel,
        out_shape=jax.ShapeDtypeStruct((2, 2, out_rows, columns, n), F32),
        in_specs=[SMEM] + [VMEM] * (1 + len(pieces)),
        out_specs=VMEM,
        scratch_shapes=[
            pltpu.VMEM((4, 3 * channels // 4, 9 * n), BF16),
            pltpu.VMEM((total, 3 * channels), BF16),
            pltpu.VMEM((total, 9 * n), F32),
        ],
        compiler_params=PARAMS,
        cost_estimate=pl.CostEstimate(flops=6 * 10**9, bytes_accessed=4 * 2**20, transcendentals=0),
    )(scalars, cache, *pieces)


def sum_taps(product, u_size, columns, n, doubled, video, frame, row):
    summed = None
    for frame_tap in range(max(0, 2 - frame), 3):
        for row_tap in range(3):
            wanted = row + row_tap
            at = (frame + frame_tap - 2) * u_size + (wanted // 2 if doubled else wanted) * columns
            at = pl.multiple_of(video * 4 * u_size + at, columns)
            lane = (3 * frame_tap + row_tap) * n
            part = product[pl.ds(at, columns), lane : lane + n]
            summed = part if summed is None else summed + part
    return summed


def first_kernel(scalar_ref, x_ref, gain_ref, held_ref, own_ref, *refs):
    pieces, (out_ref, whole, stacked, product) = refs[:-4], refs[-4:]
    set_weights(scalar_ref[1], pieces, whole)
    columns, rows, out_rows, n = 16, 5, 3, 96
    fine = spreader(columns, columns, False)

    def fill(step, carry):
        video, frame = step // 4, lax.rem(step, 4)
        for row in range(rows):
            u = normed(x_ref[video, frame, row].astype(F32), gain_ref[...])
            at = pl.multiple_of((step * rows + row) * columns, columns)
            put_taps(stacked, at, columns, dot(fine, u).astype(BF16))
        return carry

    lax.fori_loop(0, 8, fill, 0)
    multiply_all(stacked, whole, product, 8 * rows * columns)

    def add_up(video, carry):
        for frame in range(4):
            for row in range(out_rows):
                summed = sum_taps(product, rows * columns, columns, n, False, video, frame, row)
                if frame < 2:
                    summed = summed + held_ref[video, frame, row]
                summed = summed + own_ref[video, frame, row].astype(F32)
                if row == 0:
                    summed = jnp.where(scalar_ref[2] == 1, 0.0, summed)
                if row == out_rows - 1:
                    summed = jnp.where(scalar_ref[3] == 1, 0.0, summed)
                out_ref[video, frame, row] = summed.astype(BF16)
        return carry

    lax.fori_loop(0, 2, add_up, 0)


def run_first(scalars, x, gain, held, own, pieces):
    total = 8 * 5 * 16
    return pl.pallas_call(
        first_kernel,
        out_shape=jax.ShapeDtypeStruct((2, 4, 3, 16, 96), BF16),
        in_specs=[SMEM] + [VMEM] * 8,
        out_specs=VMEM,
        scratch_shapes=[
            pltpu.VMEM((4, 288, 864), BF16),
            pltpu.VMEM((total, 1152), BF16),
            pltpu.VMEM((total, 864), F32),
        ],
        compiler_params=PARAMS,
        cost_estimate=pl.CostEstimate(flops=3 * 10**9, bytes_accessed=4 * 2**20, transcendentals=0),
    )(scalars, x, gain, held, own, *pieces)


def middle_kernel(last, n_pieces, scalar_ref, gain_ref, held_ref, *refs):
    parts, pieces, refs = refs[:4], refs[4 : 4 + n_pieces], refs[4 + n_pieces :]
    if last:
        proj_ref, outs, refs = refs[0], refs[1:5], refs[5:]
    else:
        outs, refs = refs[:1], refs[1:]
    whole, inputs, active, stacked, product, shortcut = refs[:6]
    place = scalar_ref[0]
    set_weights(scalar_ref[1], pieces, whole, 0 if last else 288)
    rows, source = parts[0].shape[2], parts[0].shape[3]
    out_rows, columns, n = held_ref.shape[2], held_ref.shape[3], held_ref.shape[4]
    coarse = spreader(columns, source, True)
    middle = spreader(columns, source, True, (1,))
    frame_size = rows * source
    places = [placer(96, 384, 96 * lax.rem(place + 4 - d, 4)).astype(BF16) for d in range(4)]

    def bring(step, carry):
        video, frame = step // 4, lax.rem(step, 4)
        x = None
        for part, at in zip(parts, places):
            term = dot(part[video, frame].reshape(frame_size, 96), at)
            x = term if x is None else x + term
        if last:
            inputs[step] = x.astype(BF16).reshape(rows, source, 384)
        active[step] = normed(x, gain_ref[...]).reshape(rows, source, 384)
        return carry

    lax.fori_loop(0, 8, bring, 0)
    u_size = rows * columns

    def fill(step, carry):
        for row in range(rows):
            at = pl.multiple_of((step * rows + row) * columns, columns)
            put_taps(stacked, at, columns, dot(coarse, active[step, row]).astype(BF16))
            if last:
                own = dot(dot(middle, inputs[step, row]).astype(BF16), proj_ref[...])
            else:
                own = dot(middle, parts[0][step // 4, lax.rem(step, 4), row])
            shortcut[pl.ds(at, columns), :] = own
        return carry

    lax.fori_loop(0, 8, fill, 0)
    multiply_all(stacked, whole, product, 8 * u_size)

    def one(video, frame, row):
        summed = sum_taps(product, u_size, columns, n, True, video, frame, row)
        if frame < 2:
            summed = summed + held_ref[video, frame, row]
        at = (video * 4 + frame) * u_size + (row + 1) // 2 * columns
        summed = summed + shortcut[pl.ds(pl.multiple_of(at, columns), columns), :]
        if row == 0:
            summed = jnp.where(scalar_ref[2] == 1, 0.0, summed)
        if row == out_rows - 1:
            summed = jnp.where(scalar_ref[3] == 1, 0.0, summed)
        return summed

    if last:
        image = refs[6]
        image[0] = jnp.zeros(image.shape[1:], BF16)
        image[1] = jnp.zeros(image.shape[1:], BF16)
        for frame in range(4):
            for row in range(out_rows):
                sides = [one(0, frame, row), one(1, frame, row)]
                image[2 + frame, row] = jnp.concatenate(sides, axis=-1).astype(BF16)
        for d in range(4):
            outs[d][...] = image[pl.ds(lax.rem(place + d, 4), 3)]
        return

    def add_up(video, carry):
        for frame in range(4):
            for row in range(out_rows):
                outs[0][video, frame, row] = one(video, frame, row).astype(BF16)
        return carry

    lax.fori_loop(0, 2, add_up, 0)


def run_middle(scalars, gain, held, parts, pieces, proj=None):
    last = proj is not None
    out_rows, columns, n = held.shape[2:]
    rows, source = parts[0].shape[2:4]
    total = 8 * rows * columns
    if last:
        out_shape = [jax.ShapeDtypeStruct((3, out_rows, columns, 2 * n), BF16)] * 4
    else:
        out_shape = [jax.ShapeDtypeStruct((2, 4, out_rows, columns, n), BF16)]
    operands = [scalars, gain, held] + parts + pieces + ([proj] if last else [])
    scratch = [
        pltpu.VMEM((4, 288, 9 * n), BF16),
        pltpu.VMEM((8, rows, source, 384), BF16),
        pltpu.VMEM((8, rows, source, 384), BF16),
        pltpu.VMEM((total, 1152), BF16),
        pltpu.VMEM((total, 9 * n), F32),
        pltpu.VMEM((total, n), F32),
    ]
    if last:
        scratch.append(pltpu.VMEM((6, out_rows, columns, 2 * n), BF16))
    return pl.pallas_call(
        functools.partial(middle_kernel, last, len(pieces)),
        out_shape=out_shape,
        in_specs=[SMEM] + [VMEM] * (len(operands) - 1),
        out_specs=[VMEM] * len(out_shape),
        scratch_shapes=scratch,
        compiler_params=PARAMS,
        cost_estimate=pl.CostEstimate(flops=8 * 10**9, bytes_accessed=4 * 2**20, transcendentals=0),
    )(*operands)


def last_kernel(scalar_ref, gain_ref, cache_ref, weight_ref, proj_ref, *refs):
    parts, (out_ref, stacked, inputs, summed) = refs[:4], refs[4:]
    columns, channels, n = 128, 192, 96
    place = scalar_ref[0]
    fine = spreader(columns, columns, False)
    coarse = spreader(columns, 64, True)
    middle = spreader(columns, 64, True, (1,))
    places = []
    for d in range(4):
        lane = 48 * lax.rem(place + 4 - d, 4)
        both = placer(96, 512, lane, 0, 48) + placer(96, 512, lane + 256, 48, 96)
        places.append(both.astype(BF16))

    def put(video, frame, row, spread):
        for tap in range(3):
            stacked[video, tap, frame, row * columns : (row + 1) * columns, :] = spread[
                tap * columns : (tap + 1) * columns
            ]

    for frame in range(3):
        from_cache = place + frame < 2

        @pl.when(from_cache)
        def _():
            def one_video(video, carry):
                for row in range(10):
                    values = cache_ref[video, jnp.minimum(place + frame, 1), row]
                    put(video, frame, row, dot(fine, values).astype(BF16))
                return carry

            lax.fori_loop(0, 2, one_video, 0)

        @pl.when(jnp.logical_not(from_cache))
        def _():
            x = None
            for part, at in zip(parts, places):
                term = dot(part[frame].reshape(384, 96), at)
                x = term if x is None else x + term
            for video in range(2):
                own = x[:, 256 * video : 256 * video + channels]
                if frame == 2:
                    inputs[video] = own.astype(BF16).reshape(6, 64, channels)
                active = normed(own, gain_ref[...])
                for row in range(6):
                    spread = dot(coarse, active[64 * row : 64 * (row + 1)]).astype(BF16)
                    for copy in (2 * row - 1, 2 * row):
                        if 0 <= copy < 10:
                            put(video, frame, copy, spread)

    def one_video(video, carry):
        for row in range(8):
            if row % 2 == 0:
                own = dot(middle, inputs[video, 1 + row // 2])
                own = dot(own.astype(BF16), proj_ref[...])
            summed[row * columns : (row + 1) * columns, :] = own

        for frame_tap in range(3):
            for row_tap in range(3):
                lane = (3 * frame_tap + row_tap) * n
                part = None
                for tap in range(3):
                    term = dot(
                        stacked[video, tap, frame_tap, row_tap * columns : (row_tap + 8) * columns, :],
                        weight_ref[tap * channels : (tap + 1) * channels, lane : lane + n],
                    )
                    part = term if part is None else part + term
                summed[...] += part

        for row in range(8):
            out_ref[video, row] = summed[row * columns : (row + 1) * columns, :].T.astype(BF16)
        return carry

    lax.fori_loop(0, 2, one_video, 0)


def run_last(scalars, gain, cache, weight, proj, parts):
    return pl.pallas_call(
        last_kernel,
        out_shape=jax.ShapeDtypeStruct((2, 8, 96, 128), BF16),
        in_specs=[SMEM] + [VMEM] * 8,
        out_specs=VMEM,
        scratch_shapes=[
            pltpu.VMEM((2, 3, 3, 1280, 192), BF16),
            pltpu.VMEM((2, 6, 64, 192), BF16),
            pltpu.VMEM((1024, 96), F32),
        ],
        compiler_params=PARAMS,
        cost_estimate=pl.CostEstimate(flops=10**10, bytes_accessed=4 * 2**20, transcendentals=0),
    )(scalars, gain, cache, weight, proj, *parts)


def shards(
    features,
    cache_zero,
    cache_one,
    cache_two,
    cache_three,
    gain_zero,
    gain_one,
    gain_two,
    gain_three,
    weight_zero,
    weight_one,
    weight_two,
    weight_three,
    proj_two,
    proj_three,
):
    place = lax.axis_index("xlo") * 2 + lax.axis_index("core")
    row_at = lax.axis_index(ROWS)
    scalars = jnp.stack([place, lax.axis_index("y"), row_at == 0, row_at == 63, lax.axis_index("z")]).astype(jnp.int32)

    def quarter(x):
        width = x.shape[-1] // 4
        return lax.dynamic_slice_in_dim(x, place * width, width, x.ndim - 1)

    start = with_first_halo(jnp.concatenate([cache_zero, features], axis=1))
    mixed = jnp.concatenate([quarter(weight_two).reshape(18, 432), weight_three.reshape(18, 432)], axis=1)
    first_two = [quarter(weight).reshape(18, 864) for weight in (weight_zero, weight_one)]
    shard = jnp.concatenate(first_two + [mixed, jnp.zeros((2, 864), BF16)], axis=0)
    plane, plane2 = run_plane(scalars, ring_z(with_other_plane(shard)))
    ring = share_ring(plane)
    pieces0, pieces1 = ring[:4], ring[:3] + ring[4:]
    held_one, held_two, held_three = with_halos(cache_one, cache_two, cache_three)
    pieces2 = [lax.all_gather(plane2, "y")]

    x0 = start[:, 2:]
    before0 = run_held(scalars, start[:, :2], pieces0, 3, 96)
    own0 = run_first(scalars, x0, gain_zero[None], before0, quarter(x0[:, :, 1:4]), pieces0)
    parts1 = share_segment([own0] * 4)
    before1 = run_held(scalars, held_one, pieces1, 4, 96)
    own1 = run_middle(scalars, gain_one[None], before1, parts1, pieces1)[0]
    parts2 = share_segment([own1] * 4)
    before2 = run_held(scalars, held_two, pieces2, 6, 48)
    sent = run_middle(scalars, gain_two[None], before2, parts2, pieces2, quarter(proj_two))
    parts3 = share_segment(sent)

    w3 = run_halves(pieces2[0])
    out = run_last(scalars, gain_three[None], held_three, w3, proj_three, parts3)
    return out.transpose(0, 2, 1, 3)[:, None]


def solution(mesh):
    fine_mesh = Mesh(mesh.devices.reshape(2, 2, 4, 2, 8), ALL)
    slab = P(None, None, ROWS, None, None)
    shard = P(ROWS, None, None, None)
    return jax.shard_map(
        shards,
        mesh=fine_mesh,
        in_specs=(slab,) * 5 + (P(),) * 4 + (shard,) * 4 + (P(),) * 2,
        out_specs=P(None, SEG, None, ROWS, None),
        check_vma=False,
    )
```

```python
import functools

import jax
import jax.numpy as jnp
from jax import lax
from jax.experimental import pallas as pl
from jax.experimental.pallas import tpu as pltpu
from jax.sharding import Mesh
from jax.sharding import PartitionSpec as P

EPSILON = 1e-06
ROWS = ("y", "xhi", "z")
SEG = ("xlo", "core")
ALL = SEG + ROWS
BF16 = jnp.bfloat16
F32 = jnp.float32


def after(x, *others):
    return lax.optimization_barrier((x,) + others)[0]


def fetch_rows(x, by):
    pairs = []
    for segment in range(4):
        step = by if segment % 2 == 0 else -by
        pairs += [(segment * 64 + r + step, segment * 64 + r) for r in range(64) if 0 <= r + step < 64]
    return lax.ppermute(x, ALL, pairs)


def both_sides(own):
    core = lax.axis_index("core")
    other = lax.ppermute(own, "core", [(0, 1), (1, 0)])
    return jnp.where(core == 1, own, other), jnp.where(core == 0, own, other)


def with_halos(start, one, two, three, first_after, second_after, swap_after):
    upper = lax.axis_index("core")
    two_rows = lax.dynamic_slice_in_dim(two, upper * (two.shape[2] - 2), 2, 2)
    three_rows = lax.dynamic_slice_in_dim(three, upper * (three.shape[2] - 1), 1, 2)[:, :, 0]
    sides = jnp.concatenate([three_rows[:, 0], three_rows[:, 1]], axis=-1)
    first = after(start.reshape(-1, 384), first_after)
    second = jnp.concatenate([x.reshape(-1, 384) for x in (one, two_rows, sides)], axis=0)
    got = fetch_rows(first, 1), fetch_rows(first, 2), fetch_rows(after(second, *second_after), 1)
    got = lax.optimization_barrier(got + tuple(swap_after))[:3]
    rims = both_sides(jnp.concatenate(got, axis=0))
    nears = [rim[:192].reshape(start.shape) for rim in rims]
    fars = [rim[192:384].reshape(start.shape) for rim in rims]
    ones = [rim[384:640].reshape(2, 2, 2, 32, 384) for rim in rims]
    twos = [rim[640:1152].reshape(2, 2, 2, 64, 384) for rim in rims]
    sides = [rim[1152:].reshape(2, 128, 384) for rim in rims]
    threes = [jnp.stack([x[..., :192], x[..., 192:]], axis=1)[:, :, None] for x in sides]
    return (
        jnp.concatenate([fars[0], nears[0], start, nears[1], fars[1]], axis=2),
        jnp.concatenate([ones[0], one, ones[1]], axis=2),
        jnp.concatenate([twos[0], two, twos[1]], axis=2),
        jnp.concatenate([threes[0], three, threes[1]], axis=2),
    )


def with_other_plane(x):
    other = lax.ppermute(x, "xhi", [(0, 1), (1, 0)])
    first = lax.axis_index("xhi") == 0
    return jnp.concatenate([jnp.where(first, x, other), jnp.where(first, other, x)], axis=0)


def ring_z(mine):
    up = [(i, (i + 1) % 8) for i in range(8)]
    down = [(j, i) for i, j in up]
    half = mine.shape[0] // 2
    pieces = [mine]
    rising = falling = mine
    for step in range(1, 5):
        if step == 4:
            rising, falling = rising[:half], falling[half:]
        rising = lax.ppermute(rising, "z", up)
        falling = lax.ppermute(falling, "z", down)
        pieces += [rising, falling]
    return pieces


def share_ring(block, *wait_for):
    up = [(i, (i + 1) % 4) for i in range(4)]
    down = [(j, i) for i, j in up]
    half = block.shape[0] // 2
    sent = after(block, *wait_for) if wait_for else block
    from_below = lax.ppermute(sent, "y", up)
    from_above = lax.ppermute(sent, "y", down)
    far_top = lax.ppermute(from_below[:half], "y", up)
    far_bottom = lax.ppermute(from_above[half:], "y", down)
    return [block, from_below, from_above, far_top, far_bottom]


def share_segment(pieces):
    return [pieces[0]] + [
        lax.ppermute(pieces[d], SEG, [(i, (i + d) % 4) for i in range(4)]) for d in (1, 2, 3)
    ]


VMEM = pl.BlockSpec(memory_space=pltpu.VMEM)
SMEM = pl.BlockSpec(memory_space=pltpu.SMEM)
PARAMS = pltpu.CompilerParams(vmem_limit_bytes=44 * 2**20)


def spreader(columns, source, doubled, taps=(0, 1, 2)):
    parts = []
    for tap in taps:
        at = lax.broadcasted_iota(jnp.int32, (columns, source), 0) + (tap - 1)
        held = lax.broadcasted_iota(jnp.int32, (columns, source), 1)
        low = 2 * held if doubled else held
        high = low + 1 if doubled else low
        parts.append(jnp.where((at >= low) & (at <= high), 1.0, 0.0).astype(BF16))
    return parts[0] if len(parts) == 1 else jnp.concatenate(parts, axis=0)


def block_spreader(rows, columns, source, doubled, taps=(0, 1, 2)):
    shape = (rows * columns, rows * source)
    out = lax.broadcasted_iota(jnp.int32, shape, 0)
    held = lax.broadcasted_iota(jnp.int32, shape, 1)
    bits, held_bits = columns.bit_length() - 1, source.bit_length() - 1
    same = (out >> bits) == (held >> held_bits)
    low = held & (source - 1)
    low = 2 * low if doubled else low
    high = low + 1 if doubled else low
    parts = []
    for tap in taps:
        at = (out & (columns - 1)) + (tap - 1)
        parts.append(jnp.where(same & (at >= low) & (at <= high), 1.0, 0.0).astype(BF16))
    return parts[0] if len(parts) == 1 else jnp.concatenate(parts, axis=0)


def placer(width, lanes, offset, low=0, high=None):
    row = lax.broadcasted_iota(jnp.int32, (width, lanes), 0)
    lane = lax.broadcasted_iota(jnp.int32, (width, lanes), 1)
    hit = (lane == row - low + offset) & (row >= low) & (row < (width if high is None else high))
    return jnp.where(hit, 1.0, 0.0)


def normed(x, gain):
    scaled = x * lax.rsqrt(jnp.mean(x * x, axis=-1, keepdims=True) + EPSILON)
    scaled = scaled * gain
    return (scaled / (1.0 + jnp.exp(-scaled))).astype(BF16)


def set_weights(at, pieces, whole, base=0):
    if len(pieces) == 4:
        for piece, off in zip(pieces, (0, 3, 1, 2)):
            low = 0 if off == 2 else base
            whole[lax.rem(at + off, 4)] = piece[low : low + 288]
        return
    set_last_weights(at, pieces, whole, 0)


def set_last_weights(at, pieces, whole, lane):
    half, lanes = pieces[0].shape[0] // 2, pl.ds(lane, whole.shape[2])
    for piece, off in zip(pieces[:3], (0, 3, 1)):
        whole[lax.rem(at + off, 4)] = piece[:, lanes]
    whole[lax.rem(at + 2, 4), :half] = pieces[3][:, lanes]
    whole[lax.rem(at + 2, 4), half:] = pieces[4][:, lanes]


def put_taps(stacked, row_at, columns, spread):
    channels = spread.shape[1]
    for tap in range(3):
        stacked[pl.ds(row_at, columns), tap * channels : (tap + 1) * channels] = spread[
            tap * columns : (tap + 1) * columns
        ]


def multiply_all(stacked, whole, product, total):
    chunk = next(c for c in (512, 480, 384, 320, 256, 192, 128, 96, 64) if total % c == 0)

    def multiply(step, carry):
        at = pl.multiple_of(step * chunk, chunk)
        weight = whole[...].reshape(4 * whole.shape[1], whole.shape[2])
        product[pl.ds(at, chunk), :] = jnp.dot(
            stacked[pl.ds(at, chunk), :], weight, preferred_element_type=F32
        )
        return carry

    lax.fori_loop(0, total // chunk, multiply, 0)


def dot(a, b):
    return jnp.dot(a, b, preferred_element_type=F32)


def plane_kernel(scalar_ref, *refs):
    pieces, outs, held = refs[:9], refs[9:11], refs[11]
    at = scalar_ref[4]
    for piece, off in zip(pieces[:7], (0, 7, 1, 6, 2, 5, 3)):
        held[lax.rem(at + off, 8)] = piece[...]
    held[lax.rem(at + 4, 8), :56] = pieces[7][...]
    held[lax.rem(at + 4, 8), 56:] = pieces[8][...]
    for matrix, (out, base) in enumerate(((outs[0], 0), (outs[0], 288), (outs[1], 0))):
        for block in range(16):
            low = 56 * (block // 8) + 18 * matrix
            out[base + 18 * block : base + 18 * (block + 1), :] = held[block % 8, low : low + 18, :]


def run_plane(scalars, pieces):
    return pl.pallas_call(
        plane_kernel,
        out_shape=[jax.ShapeDtypeStruct((576, 864), BF16), jax.ShapeDtypeStruct((288, 864), BF16)],
        in_specs=[SMEM] + [VMEM] * 9,
        out_specs=[VMEM] * 2,
        scratch_shapes=[pltpu.VMEM((8, 112, 864), BF16)],
        compiler_params=PARAMS,
        cost_estimate=pl.CostEstimate(flops=10**8, bytes_accessed=4 * 2**20, transcendentals=0),
    )(scalars, *pieces)


def halves_kernel(scalar_ref, *refs):
    pieces, (out_ref, whole) = refs[:5], refs[5:]
    set_last_weights(scalar_ref[1], pieces, whole, 432)
    row = lax.broadcasted_iota(jnp.int32, (72, 144), 0)
    lane = lax.broadcasted_iota(jnp.int32, (72, 144), 1)
    picks = [jnp.where(lane == 2 * row + half, 1.0, 0.0).astype(BF16) for half in range(2)]
    for block in range(8):
        rows = whole[block // 2, 144 * (block % 2) : 144 * (block % 2 + 1), :]
        full = jnp.concatenate([dot(pick, rows) for pick in picks], axis=-1)
        for tap in range(3):
            out_ref[tap, 72 * block : 72 * (block + 1), :] = full[:, 288 * tap : 288 * (tap + 1)].astype(BF16)


def run_halves(scalars, pieces):
    return pl.pallas_call(
        halves_kernel,
        out_shape=jax.ShapeDtypeStruct((3, 576, 288), BF16),
        in_specs=[SMEM] + [VMEM] * 5,
        out_specs=VMEM,
        scratch_shapes=[pltpu.VMEM((4, 288, 432), BF16)],
        compiler_params=PARAMS,
        cost_estimate=pl.CostEstimate(flops=10**8, bytes_accessed=4 * 2**20, transcendentals=0),
    )(scalars, *pieces)


def held_kernel(scalar_ref, cache_ref, *refs):
    pieces, (out_ref, whole, stacked, product) = refs[:-4], refs[-4:]
    rows, columns = cache_ref.shape[2], cache_ref.shape[3]
    out_rows, n = out_ref.shape[2], out_ref.shape[4]
    set_weights(scalar_ref[1], pieces, whole, 0 if columns == 16 else 288)
    fine = spreader(columns, columns, False)
    size = rows * columns

    def fill(frame, carry):
        for row in range(rows):
            at = pl.multiple_of(frame * size + row * columns, columns)
            values = cache_ref[frame // 2, lax.rem(frame, 2), row]
            put_taps(stacked, at, columns, dot(fine, values).astype(BF16))
        return carry

    lax.fori_loop(0, 4, fill, 0)
    multiply_all(stacked, whole, product, 4 * size)

    def add_up(video, carry):
        for frame in range(2):
            for row in range(out_rows):
                summed = None
                for frame_tap in range(2 - frame):
                    for row_tap in range(3):
                        at = (frame + frame_tap) * size + (row + row_tap) * columns
                        at = pl.multiple_of(video * 2 * size + at, columns)
                        lane = (3 * frame_tap + row_tap) * n
                        part = product[pl.ds(at, columns), lane : lane + n]
                        summed = part if summed is None else summed + part
                out_ref[video, frame, row] = summed
        return carry

    lax.fori_loop(0, 2, add_up, 0)


def run_held(scalars, cache, pieces, out_rows, n):
    rows, columns, channels = cache.shape[2:]
    total = 4 * rows * columns
    return pl.pallas_call(
        held_kernel,
        out_shape=jax.ShapeDtypeStruct((2, 2, out_rows, columns, n), F32),
        in_specs=[SMEM] + [VMEM] * (1 + len(pieces)),
        out_specs=VMEM,
        scratch_shapes=[
            pltpu.VMEM((4, 3 * channels // 4, 9 * n), BF16),
            pltpu.VMEM((total, 3 * channels), BF16),
            pltpu.VMEM((total, 9 * n), F32),
        ],
        compiler_params=PARAMS,
        cost_estimate=pl.CostEstimate(flops=6 * 10**9, bytes_accessed=4 * 2**20, transcendentals=0),
    )(scalars, cache, *pieces)


def first_kernel(scalar_ref, x_ref, gain_ref, own_ref, *refs):
    pieces, (out_ref, whole, stacked, product) = refs[:-4], refs[-4:]
    set_weights(scalar_ref[1], pieces, whole)
    columns, rows, out_rows, n = 16, 5, 3, 96
    size = rows * columns
    fine = block_spreader(8, columns, columns, False)

    def fill(video, carry):
        for frame in range(6):
            u = x_ref[video, frame].reshape(size, 384)
            if frame >= 2:
                u = normed(u.astype(F32), gain_ref[...])
            at = pl.multiple_of((video * 6 + frame) * size, size)
            for tap in range(3):
                part = fine[128 * tap : 128 * tap + size, :size]
                stacked[pl.ds(at, size), 384 * tap : 384 * (tap + 1)] = dot(part, u).astype(BF16)
        return carry

    lax.fori_loop(0, 2, fill, 0)
    multiply_all(stacked, whole, product, 12 * size)

    def add_up(video, carry):
        for frame in range(4):
            for row in range(out_rows):
                summed = own_ref[video, frame, row].astype(F32)
                for frame_tap in range(3):
                    for row_tap in range(3):
                        at = (video * 6 + frame + frame_tap) * size + (row + row_tap) * columns
                        lane = (3 * frame_tap + row_tap) * n
                        summed = summed + product[pl.ds(pl.multiple_of(at, columns), columns), lane : lane + n]
                if row == 0:
                    summed = jnp.where(scalar_ref[2] == 1, 0.0, summed)
                if row == out_rows - 1:
                    summed = jnp.where(scalar_ref[3] == 1, 0.0, summed)
                out_ref[video, frame, row] = summed.astype(BF16)
        return carry

    lax.fori_loop(0, 2, add_up, 0)


def run_first(scalars, x, gain, own, pieces):
    total = 12 * 5 * 16
    return pl.pallas_call(
        first_kernel,
        out_shape=jax.ShapeDtypeStruct((2, 4, 3, 16, 96), BF16),
        in_specs=[SMEM] + [VMEM] * 7,
        out_specs=VMEM,
        scratch_shapes=[
            pltpu.VMEM((4, 288, 864), BF16),
            pltpu.VMEM((total, 1152), BF16),
            pltpu.VMEM((total, 864), F32),
        ],
        compiler_params=PARAMS,
        cost_estimate=pl.CostEstimate(flops=3 * 10**9, bytes_accessed=4 * 2**20, transcendentals=0),
    )(scalars, x, gain, own, *pieces)


def middle_kernel(last, n_pieces, scalar_ref, gain_ref, held_ref, *refs):
    parts, pieces, refs = refs[:4], refs[4 : 4 + n_pieces], refs[4 + n_pieces :]
    if last:
        proj_ref, outs, refs = refs[0], refs[1:5], refs[5:]
    else:
        outs, refs = refs[:1], refs[1:]
    whole, stacked, product, shortcut = refs[:4]
    place = scalar_ref[0]
    set_weights(scalar_ref[1], pieces, whole, 0 if last else 288)
    rows, source = parts[0].shape[2], parts[0].shape[3]
    out_rows, columns, n = held_ref.shape[2], held_ref.shape[3], held_ref.shape[4]
    coarse = block_spreader(rows, columns, source, True)
    middle = block_spreader(rows, columns, source, True, (1,))
    frame_size, u_size = rows * source, rows * columns
    places = [placer(96, 384, 96 * lax.rem(place + 4 - d, 4)).astype(BF16) for d in range(4)]

    def fill(step, carry):
        video, frame = step // 4, lax.rem(step, 4)
        x = None
        for part, at in zip(parts, places):
            term = dot(part[video, frame].reshape(frame_size, 96), at)
            x = term if x is None else x + term
        spread = dot(coarse, normed(x, gain_ref[...])).astype(BF16)
        at = pl.ds(pl.multiple_of(step * u_size, u_size), u_size)
        for tap in range(3):
            stacked[at, tap * 384 : (tap + 1) * 384] = spread[tap * u_size : (tap + 1) * u_size]
        if last:
            own = dot(dot(middle, x.astype(BF16)).astype(BF16), proj_ref[...])
        else:
            own = dot(middle, parts[0][video, frame].reshape(frame_size, 96))
        shortcut[at, :] = own
        return carry

    lax.fori_loop(0, 8, fill, 0, unroll=2)
    multiply_all(stacked, whole, product, 8 * u_size)

    def one_frame(video, frame):
        sums = []
        for row in range(rows):
            for row_tap in range(3):
                summed = None
                for frame_tap in range(max(0, 2 - frame), 3):
                    at = (video * 4 + frame + frame_tap - 2) * u_size + row * columns
                    lane = (3 * frame_tap + row_tap) * n
                    part = product[pl.ds(pl.multiple_of(at, columns), columns), lane : lane + n]
                    summed = part if summed is None else summed + part
                sums.append(summed)
        outcomes = []
        for row in range(out_rows):
            at = (video * 4 + frame) * u_size + (row + 1) // 2 * columns
            summed = shortcut[pl.ds(pl.multiple_of(at, columns), columns), :]
            for row_tap in range(3):
                summed = summed + sums[3 * ((row + row_tap) // 2) + row_tap]
            if frame < 2:
                summed = summed + held_ref[video, frame, row]
            if row == 0:
                summed = jnp.where(scalar_ref[2] == 1, 0.0, summed)
            if row == out_rows - 1:
                summed = jnp.where(scalar_ref[3] == 1, 0.0, summed)
            outcomes.append(summed)
        return outcomes

    if last:
        image = refs[4]
        image[0] = jnp.zeros(image.shape[1:], BF16)
        image[1] = jnp.zeros(image.shape[1:], BF16)
        for frame in range(4):
            for row, sides in enumerate(zip(one_frame(0, frame), one_frame(1, frame))):
                image[2 + frame, row] = jnp.concatenate(sides, axis=-1).astype(BF16)
        for d in range(4):
            outs[d][...] = image[pl.ds(lax.rem(place + d, 4), 3)]
        return

    def add_up(video, carry):
        for frame in range(4):
            for row, summed in enumerate(one_frame(video, frame)):
                outs[0][video, frame, row] = summed.astype(BF16)
        return carry

    lax.fori_loop(0, 2, add_up, 0)


def run_middle(scalars, gain, held, parts, pieces, proj=None):
    last = proj is not None
    out_rows, columns, n = held.shape[2:]
    rows, source = parts[0].shape[2:4]
    total = 8 * rows * columns
    if last:
        out_shape = [jax.ShapeDtypeStruct((3, out_rows, columns, 2 * n), BF16)] * 4
    else:
        out_shape = [jax.ShapeDtypeStruct((2, 4, out_rows, columns, n), BF16)]
    operands = [scalars, gain, held] + parts + pieces + ([proj] if last else [])
    scratch = [
        pltpu.VMEM((4, 288, 9 * n), BF16),
        pltpu.VMEM((total, 1152), BF16),
        pltpu.VMEM((total, 9 * n), F32),
        pltpu.VMEM((total, n), F32),
    ]
    if last:
        scratch.append(pltpu.VMEM((6, out_rows, columns, 2 * n), BF16))
    return pl.pallas_call(
        functools.partial(middle_kernel, last, len(pieces)),
        out_shape=out_shape,
        in_specs=[SMEM] + [VMEM] * (len(operands) - 1),
        out_specs=[VMEM] * len(out_shape),
        scratch_shapes=scratch,
        compiler_params=PARAMS,
        cost_estimate=pl.CostEstimate(flops=8 * 10**9, bytes_accessed=4 * 2**20, transcendentals=0),
    )(*operands)


def last_held_kernel(scalar_ref, cache_ref, weight_ref, out_ref, stacked):
    columns, channels, n = 128, 192, 96
    place = scalar_ref[0]
    fine = spreader(columns, columns, False)
    out_ref[...] = jnp.zeros(out_ref.shape, F32)

    def one_video(video, carry):
        for frame in range(2):

            @pl.when(place + frame < 2)
            def _():
                for row in range(10):
                    values = cache_ref[video, jnp.minimum(place + frame, 1), row]
                    spread = dot(fine, values).astype(BF16)
                    for tap in range(3):
                        stacked[tap, row * columns : (row + 1) * columns, :] = spread[
                            tap * columns : (tap + 1) * columns
                        ]
                for row_tap in range(3):
                    part = None
                    for tap in range(3):
                        term = dot(
                            stacked[tap, row_tap * columns : (row_tap + 8) * columns, :],
                            weight_ref[frame, tap * channels : (tap + 1) * channels, n * row_tap : n * (row_tap + 1)],
                        )
                        part = term if part is None else part + term
                    out_ref[video] += part

        return carry

    lax.fori_loop(0, 2, one_video, 0)


def run_last_held(scalars, cache, weight):
    return pl.pallas_call(
        last_held_kernel,
        out_shape=jax.ShapeDtypeStruct((2, 1024, 96), F32),
        in_specs=[SMEM] + [VMEM] * 2,
        out_specs=VMEM,
        scratch_shapes=[pltpu.VMEM((3, 1280, 192), BF16)],
        compiler_params=PARAMS,
        cost_estimate=pl.CostEstimate(flops=8 * 10**9, bytes_accessed=4 * 2**20, transcendentals=0),
    )(scalars, cache, weight)


def last_kernel(scalar_ref, gain_ref, held_ref, weight_ref, proj_ref, *refs):
    parts, (out_ref, stacked, summed) = refs[:4], refs[4:]
    columns, channels, n = 128, 192, 96
    place = scalar_ref[0]
    coarse = spreader(columns, 64, True)
    middle = spreader(columns, 64, True, (1,))
    places = []
    for d in range(4):
        lane = 48 * lax.rem(place + 4 - d, 4)
        both = placer(96, 512, lane, 0, 48) + placer(96, 512, lane + 256, 48, 96)
        places.append(both.astype(BF16))

    for frame in (2, 1, 0):

        @pl.when(place + frame >= 2)
        def _():
            x = None
            for part, at in zip(parts, places):
                term = dot(part[frame].reshape(384, 96), at)
                x = term if x is None else x + term
            for video in range(2):
                own = x[:, 256 * video : 256 * video + channels]
                if frame == 2:
                    inputs = own.astype(BF16)
                    for row in range(4):
                        side = dot(middle, inputs[64 * (row + 1) : 64 * (row + 2)]).astype(BF16)
                        side = dot(side, proj_ref[...])
                        for copy in (2 * row, 2 * row + 1):
                            low = copy * columns
                            summed[video, low : low + columns, :] = side + held_ref[video, low : low + columns, :]
                active = normed(own, gain_ref[...])
                for row in range(6):
                    spread = dot(coarse, active[64 * row : 64 * (row + 1)]).astype(BF16)
                    for tap in range(3):
                        stacked[video, tap, row * columns : (row + 1) * columns, :] = spread[
                            tap * columns : (tap + 1) * columns
                        ]
            for video in range(2):
                product = None
                for tap in range(3):
                    term = dot(
                        stacked[video, tap],
                        weight_ref[frame, tap * channels : (tap + 1) * channels, :],
                    )
                    product = term if product is None else product + term
                for row in range(8):
                    part = None
                    for row_tap in range(3):
                        held_row = (row + row_tap + 1) // 2
                        term = product[
                            held_row * columns : (held_row + 1) * columns, n * row_tap : n * (row_tap + 1)
                        ]
                        part = term if part is None else part + term
                    summed[video, row * columns : (row + 1) * columns, :] += part

    for video in range(2):
        for row in range(8):
            out_ref[video, row] = summed[video, row * columns : (row + 1) * columns, :].T.astype(BF16)


def run_last(scalars, gain, held, weight, proj, parts):
    return pl.pallas_call(
        last_kernel,
        out_shape=jax.ShapeDtypeStruct((2, 8, 96, 128), BF16),
        in_specs=[SMEM] + [VMEM] * 8,
        out_specs=VMEM,
        scratch_shapes=[
            pltpu.VMEM((2, 3, 768, 192), BF16),
            pltpu.VMEM((2, 1024, 96), F32),
        ],
        compiler_params=PARAMS,
        cost_estimate=pl.CostEstimate(flops=10**10, bytes_accessed=4 * 2**20, transcendentals=0),
    )(scalars, gain, held, weight, proj, *parts)


def shards(
    features,
    cache_zero,
    cache_one,
    cache_two,
    cache_three,
    gain_zero,
    gain_one,
    gain_two,
    gain_three,
    weight_zero,
    weight_one,
    weight_two,
    weight_three,
    proj_two,
    proj_three,
):
    place = lax.axis_index("xlo") * 2 + lax.axis_index("core")
    row_at = lax.axis_index(ROWS)
    scalars = jnp.stack([place, lax.axis_index("y"), row_at == 0, row_at == 63, lax.axis_index("z")]).astype(jnp.int32)

    def quarter(x):
        width = x.shape[-1] // 4
        return lax.dynamic_slice_in_dim(x, place * width, width, x.ndim - 1)

    mixed = jnp.concatenate([quarter(weight_two).reshape(18, 432), weight_three.reshape(18, 432)], axis=1)
    first_two = [quarter(weight).reshape(18, 864) for weight in (weight_zero, weight_one)]
    shard = jnp.concatenate(first_two + [mixed, jnp.zeros((2, 864), BF16)], axis=0)
    plane, plane2 = run_plane(scalars, ring_z(with_other_plane(shard)))
    ring = share_ring(plane)
    pieces0, pieces1 = ring[:4], ring[:3] + ring[4:]
    start, held_one, held_two, held_three = with_halos(
        jnp.concatenate([cache_zero, features], axis=1),
        cache_one,
        cache_two,
        cache_three,
        plane,
        ring[1:3],
        ring[3:],
    )

    own0 = run_first(scalars, start, gain_zero[None], quarter(start[:, 2:, 1:4]), pieces0)
    parts1 = share_segment([own0] * 4)
    pieces2 = share_ring(plane2, own0)
    before1 = run_held(scalars, held_one, pieces1, 4, 96)
    own1 = run_middle(scalars, gain_one[None], before1, parts1, pieces1)[0]
    parts2 = share_segment([own1] * 4)
    before2 = run_held(scalars, held_two, pieces2, 6, 48)
    sent = run_middle(scalars, gain_two[None], before2, parts2, pieces2, quarter(proj_two))
    parts3 = share_segment(sent)

    w3 = run_halves(scalars, pieces2)
    before3 = run_last_held(scalars, held_three, w3)
    out = run_last(scalars, gain_three[None], before3, w3, proj_three, parts3)
    return out.transpose(0, 2, 1, 3)[:, None]


def solution(mesh):
    fine_mesh = Mesh(mesh.devices.reshape(2, 2, 4, 2, 8), ALL)
    slab = P(None, None, ROWS, None, None)
    shard = P(ROWS, None, None, None)
    return jax.shard_map(
        shards,
        mesh=fine_mesh,
        in_specs=(slab,) * 5 + (P(),) * 4 + (shard,) * 4 + (P(),) * 2,
        out_specs=P(None, SEG, None, ROWS, None),
        check_vma=False,
    )
```

```python
import functools

import jax
import jax.numpy as jnp
from jax import lax
from jax.experimental import pallas as pl
from jax.experimental.pallas import tpu as pltpu
from jax.sharding import Mesh
from jax.sharding import PartitionSpec as P

EPSILON = 1e-06
ROWS = ("y", "xhi", "z")
SEG = ("xlo", "core")
ALL = SEG + ROWS
BF16 = jnp.bfloat16
F32 = jnp.float32


def after(x, *others):
    return lax.optimization_barrier((x,) + others)[0]


def fetch_rows(x, by):
    pairs = []
    for segment in range(4):
        step = by if segment % 2 == 0 else -by
        pairs += [(segment * 64 + r + step, segment * 64 + r) for r in range(64) if 0 <= r + step < 64]
    return lax.ppermute(x, ALL, pairs)


def sides_of(own, other):
    core = lax.axis_index("core")
    return jnp.where(core == 1, own, other), jnp.where(core == 0, own, other)


def with_halos(start, one, two, three, first_after, second_after, swap_after):
    upper = lax.axis_index("core")
    two_rows = lax.dynamic_slice_in_dim(two, upper * (two.shape[2] - 2), 2, 2)
    three_rows = lax.dynamic_slice_in_dim(three, upper * (three.shape[2] - 1), 1, 2)[:, :, 0]
    sides = jnp.concatenate([three_rows[:, 0], three_rows[:, 1]], axis=-1)
    first = after(start.reshape(-1, 384), first_after)
    second = jnp.concatenate([x.reshape(-1, 384) for x in (one, two_rows, sides)], axis=0)
    got = fetch_rows(first, 1), fetch_rows(first, 2), fetch_rows(after(second, *second_after), 1)
    got = lax.optimization_barrier(got + tuple(swap_after))[:3]
    own = jnp.concatenate(got, axis=0)
    other = lax.ppermute(own, "core", [(0, 1), (1, 0)])
    rims = sides_of(own[:384], other[:384])
    nears = [rim[:192].reshape(start.shape) for rim in rims]
    fars = [rim[192:].reshape(start.shape) for rim in rims]
    return jnp.concatenate([fars[0], nears[0], start, nears[1], fars[1]], axis=2), (own, other)


def later_halos(swapped, one, two, three, wait_for):
    own, other, one, two, three = lax.optimization_barrier(swapped + (one, two, three, wait_for))[:5]
    rims = sides_of(own[384:], other[384:])
    ones = [rim[:256].reshape(2, 2, 2, 32, 384) for rim in rims]
    twos = [rim[256:768].reshape(2, 2, 2, 64, 384) for rim in rims]
    sides = [rim[768:].reshape(2, 128, 384) for rim in rims]
    threes = [jnp.stack([x[..., :192], x[..., 192:]], axis=1)[:, :, None] for x in sides]
    return (
        jnp.concatenate([ones[0], one, ones[1]], axis=2),
        jnp.concatenate([twos[0], two, twos[1]], axis=2),
        jnp.concatenate([threes[0], three, threes[1]], axis=2),
    )


def with_other_plane(x):
    other = lax.ppermute(x, "xhi", [(0, 1), (1, 0)])
    first = lax.axis_index("xhi") == 0
    return jnp.concatenate([jnp.where(first, x, other), jnp.where(first, other, x)], axis=0)


def ring_z(mine):
    up = [(i, (i + 1) % 8) for i in range(8)]
    down = [(j, i) for i, j in up]
    half = mine.shape[0] // 2
    pieces = [mine]
    rising = falling = mine
    for step in range(1, 5):
        if step == 4:
            rising, falling = rising[:half], falling[half:]
        rising = lax.ppermute(rising, "z", up)
        falling = lax.ppermute(falling, "z", down)
        pieces += [rising, falling]
    return pieces


def share_ring(block, *wait_for):
    up = [(i, (i + 1) % 4) for i in range(4)]
    down = [(j, i) for i, j in up]
    half = block.shape[0] // 2
    sent = after(block, *wait_for) if wait_for else block
    from_below = lax.ppermute(sent, "y", up)
    from_above = lax.ppermute(sent, "y", down)
    far_top = lax.ppermute(from_below[:half], "y", up)
    far_bottom = lax.ppermute(from_above[half:], "y", down)
    return [block, from_below, from_above, far_top, far_bottom]


def share_column(block):
    return [block] + [
        lax.ppermute(block, "y", [(i, (i + d) % 4) for i in range(4)]) for d in (1, 3, 2)
    ]


def share_segment(pieces):
    return [pieces[0]] + [
        lax.ppermute(pieces[d], SEG, [(i, (i + d) % 4) for i in range(4)]) for d in (1, 2, 3)
    ]


VMEM = pl.BlockSpec(memory_space=pltpu.VMEM)
SMEM = pl.BlockSpec(memory_space=pltpu.SMEM)
PARAMS = pltpu.CompilerParams(vmem_limit_bytes=44 * 2**20)


def spreader(columns, source, doubled, taps=(0, 1, 2)):
    parts = []
    for tap in taps:
        at = lax.broadcasted_iota(jnp.int32, (columns, source), 0) + (tap - 1)
        held = lax.broadcasted_iota(jnp.int32, (columns, source), 1)
        low = 2 * held if doubled else held
        high = low + 1 if doubled else low
        parts.append(jnp.where((at >= low) & (at <= high), 1.0, 0.0).astype(BF16))
    return parts[0] if len(parts) == 1 else jnp.concatenate(parts, axis=0)


def block_spreader(rows, columns, source, doubled, taps=(0, 1, 2)):
    shape = (rows * columns, rows * source)
    out = lax.broadcasted_iota(jnp.int32, shape, 0)
    held = lax.broadcasted_iota(jnp.int32, shape, 1)
    bits, held_bits = columns.bit_length() - 1, source.bit_length() - 1
    same = (out >> bits) == (held >> held_bits)
    low = held & (source - 1)
    low = 2 * low if doubled else low
    high = low + 1 if doubled else low
    parts = []
    for tap in taps:
        at = (out & (columns - 1)) + (tap - 1)
        parts.append(jnp.where(same & (at >= low) & (at <= high), 1.0, 0.0).astype(BF16))
    return parts[0] if len(parts) == 1 else jnp.concatenate(parts, axis=0)


def placer(width, lanes, offset, low=0, high=None):
    row = lax.broadcasted_iota(jnp.int32, (width, lanes), 0)
    lane = lax.broadcasted_iota(jnp.int32, (width, lanes), 1)
    hit = (lane == row - low + offset) & (row >= low) & (row < (width if high is None else high))
    return jnp.where(hit, 1.0, 0.0)


def normed(x, gain):
    scaled = x * lax.rsqrt(jnp.mean(x * x, axis=-1, keepdims=True) + EPSILON)
    scaled = scaled * gain
    return (scaled / (1.0 + jnp.exp(-scaled))).astype(BF16)


def set_weights(at, pieces, whole, base=0):
    for piece, off in zip(pieces, (0, 3, 1, 2)):
        low = 0 if off == 2 else base
        whole[lax.rem(at + off, 4)] = piece[low : low + 288]


def set_last_weights(at, pieces, whole, lane):
    lanes = pl.ds(lane, whole.shape[2])
    for piece, off in zip(pieces, (0, 3, 1, 2)):
        whole[lax.rem(at + off, 4)] = piece[:, lanes]


def put_taps(stacked, row_at, columns, spread):
    channels = spread.shape[1]
    for tap in range(3):
        stacked[pl.ds(row_at, columns), tap * channels : (tap + 1) * channels] = spread[
            tap * columns : (tap + 1) * columns
        ]


def multiply_all(stacked, whole, product, total):
    chunk = next(c for c in (512, 480, 384, 320, 256, 192, 128, 96, 64) if total % c == 0)

    def multiply(step, carry):
        at = pl.multiple_of(step * chunk, chunk)
        weight = whole[...].reshape(4 * whole.shape[1], whole.shape[2])
        product[pl.ds(at, chunk), :] = jnp.dot(
            stacked[pl.ds(at, chunk), :], weight, preferred_element_type=F32
        )
        return carry

    lax.fori_loop(0, total // chunk, multiply, 0)


def dot(a, b):
    return jnp.dot(a, b, preferred_element_type=F32)


def plane_kernel(scalar_ref, *refs):
    pieces, outs, held = refs[:9], refs[9:11], refs[11]
    at = scalar_ref[4]
    for piece, off in zip(pieces[:7], (0, 7, 1, 6, 2, 5, 3)):
        held[lax.rem(at + off, 8)] = piece[...]
    held[lax.rem(at + 4, 8), :56] = pieces[7][...]
    held[lax.rem(at + 4, 8), 56:] = pieces[8][...]
    for matrix, (out, base) in enumerate(((outs[0], 0), (outs[0], 288), (outs[1], 0))):
        for block in range(16):
            low = 56 * (block // 8) + 18 * matrix
            out[base + 18 * block : base + 18 * (block + 1), :] = held[block % 8, low : low + 18, :]


def run_plane(scalars, pieces):
    return pl.pallas_call(
        plane_kernel,
        out_shape=[jax.ShapeDtypeStruct((576, 864), BF16), jax.ShapeDtypeStruct((288, 864), BF16)],
        in_specs=[SMEM] + [VMEM] * 9,
        out_specs=[VMEM] * 2,
        scratch_shapes=[pltpu.VMEM((8, 112, 864), BF16)],
        compiler_params=PARAMS,
        cost_estimate=pl.CostEstimate(flops=10**8, bytes_accessed=4 * 2**20, transcendentals=0),
    )(scalars, *pieces)


def halves_kernel(scalar_ref, *refs):
    pieces, (out_ref, whole) = refs[:4], refs[4:]
    set_last_weights(scalar_ref[1], pieces, whole, 432)
    row = lax.broadcasted_iota(jnp.int32, (72, 144), 0)
    lane = lax.broadcasted_iota(jnp.int32, (72, 144), 1)
    picks = [jnp.where(lane == 2 * row + half, 1.0, 0.0).astype(BF16) for half in range(2)]
    for block in range(8):
        rows = whole[block // 2, 144 * (block % 2) : 144 * (block % 2 + 1), :]
        full = jnp.concatenate([dot(pick, rows) for pick in picks], axis=-1)
        for tap in range(3):
            out_ref[tap, 72 * block : 72 * (block + 1), :] = full[:, 288 * tap : 288 * (tap + 1)].astype(BF16)


def run_halves(scalars, pieces):
    return pl.pallas_call(
        halves_kernel,
        out_shape=jax.ShapeDtypeStruct((3, 576, 288), BF16),
        in_specs=[SMEM] + [VMEM] * 4,
        out_specs=VMEM,
        scratch_shapes=[pltpu.VMEM((4, 288, 432), BF16)],
        compiler_params=PARAMS,
        cost_estimate=pl.CostEstimate(flops=10**8, bytes_accessed=4 * 2**20, transcendentals=0),
    )(scalars, *pieces)


def held_kernel(scalar_ref, cache_ref, *refs):
    pieces, (out_ref, whole, stacked, product) = refs[:-4], refs[-4:]
    rows, columns = cache_ref.shape[2], cache_ref.shape[3]
    out_rows, n = out_ref.shape[2], out_ref.shape[4]
    if n == 96:
        set_weights(scalar_ref[1], pieces, whole, 288)
    else:
        set_last_weights(scalar_ref[1], pieces, whole, 0)
    fine = spreader(columns, columns, False)
    size = rows * columns

    def fill(frame, carry):
        for row in range(rows):
            at = pl.multiple_of(frame * size + row * columns, columns)
            values = cache_ref[frame // 2, lax.rem(frame, 2), row]
            put_taps(stacked, at, columns, dot(fine, values).astype(BF16))
        return carry

    lax.fori_loop(0, 4, fill, 0)
    multiply_all(stacked, whole, product, 4 * size)

    def add_up(video, carry):
        for frame in range(2):
            for row in range(out_rows):
                summed = None
                for frame_tap in range(2 - frame):
                    for row_tap in range(3):
                        at = (frame + frame_tap) * size + (row + row_tap) * columns
                        at = pl.multiple_of(video * 2 * size + at, columns)
                        lane = (3 * frame_tap + row_tap) * n
                        part = product[pl.ds(at, columns), lane : lane + n]
                        summed = part if summed is None else summed + part
                out_ref[video, frame, row] = summed
        return carry

    lax.fori_loop(0, 2, add_up, 0)


def run_held(scalars, cache, pieces, out_rows, n):
    rows, columns, channels = cache.shape[2:]
    total = 4 * rows * columns
    return pl.pallas_call(
        held_kernel,
        out_shape=jax.ShapeDtypeStruct((2, 2, out_rows, columns, n), F32),
        in_specs=[SMEM] + [VMEM] * (1 + len(pieces)),
        out_specs=VMEM,
        scratch_shapes=[
            pltpu.VMEM((4, 3 * channels // 4, 9 * n), BF16),
            pltpu.VMEM((total, 3 * channels), BF16),
            pltpu.VMEM((total, 9 * n), F32),
        ],
        compiler_params=PARAMS,
        cost_estimate=pl.CostEstimate(flops=6 * 10**9, bytes_accessed=4 * 2**20, transcendentals=0),
    )(scalars, cache, *pieces)


def first_kernel(scalar_ref, x_ref, gain_ref, own_ref, *refs):
    pieces, (out_ref, whole, stacked, product) = refs[:-4], refs[-4:]
    set_weights(scalar_ref[1], pieces, whole)
    columns, rows, out_rows, n = 16, 5, 3, 96
    size = rows * columns
    fine = block_spreader(8, columns, columns, False)

    def fill(video, carry):
        for frame in range(6):
            u = x_ref[video, frame].reshape(size, 384)
            if frame >= 2:
                u = normed(u.astype(F32), gain_ref[...])
            at = pl.multiple_of((video * 6 + frame) * size, size)
            for tap in range(3):
                part = fine[128 * tap : 128 * tap + size, :size]
                stacked[pl.ds(at, size), 384 * tap : 384 * (tap + 1)] = dot(part, u).astype(BF16)
        return carry

    lax.fori_loop(0, 2, fill, 0)
    multiply_all(stacked, whole, product, 12 * size)

    def add_up(video, carry):
        for frame in range(4):
            for row in range(out_rows):
                summed = own_ref[video, frame, row].astype(F32)
                for frame_tap in range(3):
                    for row_tap in range(3):
                        at = (video * 6 + frame + frame_tap) * size + (row + row_tap) * columns
                        lane = (3 * frame_tap + row_tap) * n
                        summed = summed + product[pl.ds(pl.multiple_of(at, columns), columns), lane : lane + n]
                if row == 0:
                    summed = jnp.where(scalar_ref[2] == 1, 0.0, summed)
                if row == out_rows - 1:
                    summed = jnp.where(scalar_ref[3] == 1, 0.0, summed)
                out_ref[video, frame, row] = summed.astype(BF16)
        return carry

    lax.fori_loop(0, 2, add_up, 0)


def run_first(scalars, x, gain, own, pieces):
    total = 12 * 5 * 16
    return pl.pallas_call(
        first_kernel,
        out_shape=jax.ShapeDtypeStruct((2, 4, 3, 16, 96), BF16),
        in_specs=[SMEM] + [VMEM] * 7,
        out_specs=VMEM,
        scratch_shapes=[
            pltpu.VMEM((4, 288, 864), BF16),
            pltpu.VMEM((total, 1152), BF16),
            pltpu.VMEM((total, 864), F32),
        ],
        compiler_params=PARAMS,
        cost_estimate=pl.CostEstimate(flops=3 * 10**9, bytes_accessed=4 * 2**20, transcendentals=0),
    )(scalars, x, gain, own, *pieces)


def middle_kernel(last, n_pieces, scalar_ref, gain_ref, held_ref, *refs):
    parts, pieces, refs = refs[:4], refs[4 : 4 + n_pieces], refs[4 + n_pieces :]
    if last:
        proj_ref, outs, refs = refs[0], refs[1:5], refs[5:]
    else:
        outs, refs = refs[:1], refs[1:]
    whole, stacked, product, shortcut = refs[:4]
    place = scalar_ref[0]
    if last:
        set_last_weights(scalar_ref[1], pieces, whole, 0)
    else:
        set_weights(scalar_ref[1], pieces, whole, 288)
    rows, source = parts[0].shape[2], parts[0].shape[3]
    out_rows, columns, n = held_ref.shape[2], held_ref.shape[3], held_ref.shape[4]
    coarse = block_spreader(rows, columns, source, True)
    middle = block_spreader(rows, columns, source, True, (1,))
    frame_size, u_size = rows * source, rows * columns
    places = [placer(96, 384, 96 * lax.rem(place + 4 - d, 4)).astype(BF16) for d in range(4)]

    def fill(step, carry):
        video, frame = step // 4, lax.rem(step, 4)
        x = None
        for part, at in zip(parts, places):
            term = dot(part[video, frame].reshape(frame_size, 96), at)
            x = term if x is None else x + term
        spread = dot(coarse, normed(x, gain_ref[...])).astype(BF16)
        at = pl.ds(pl.multiple_of(step * u_size, u_size), u_size)
        for tap in range(3):
            stacked[at, tap * 384 : (tap + 1) * 384] = spread[tap * u_size : (tap + 1) * u_size]
        if last:
            own = dot(dot(middle, x.astype(BF16)).astype(BF16), proj_ref[...])
        else:
            own = dot(middle, parts[0][video, frame].reshape(frame_size, 96))
        shortcut[at, :] = own
        return carry

    lax.fori_loop(0, 8, fill, 0, unroll=2)
    multiply_all(stacked, whole, product, 8 * u_size)

    def one_frame(video, frame):
        sums = []
        for row in range(rows):
            for row_tap in range(3):
                summed = None
                for frame_tap in range(max(0, 2 - frame), 3):
                    at = (video * 4 + frame + frame_tap - 2) * u_size + row * columns
                    lane = (3 * frame_tap + row_tap) * n
                    part = product[pl.ds(pl.multiple_of(at, columns), columns), lane : lane + n]
                    summed = part if summed is None else summed + part
                sums.append(summed)
        outcomes = []
        for row in range(out_rows):
            at = (video * 4 + frame) * u_size + (row + 1) // 2 * columns
            summed = shortcut[pl.ds(pl.multiple_of(at, columns), columns), :]
            for row_tap in range(3):
                summed = summed + sums[3 * ((row + row_tap) // 2) + row_tap]
            if frame < 2:
                summed = summed + held_ref[video, frame, row]
            if row == 0:
                summed = jnp.where(scalar_ref[2] == 1, 0.0, summed)
            if row == out_rows - 1:
                summed = jnp.where(scalar_ref[3] == 1, 0.0, summed)
            outcomes.append(summed)
        return outcomes

    if last:
        image = refs[4]
        image[0] = jnp.zeros(image.shape[1:], BF16)
        image[1] = jnp.zeros(image.shape[1:], BF16)
        for frame in range(4):
            for row, sides in enumerate(zip(one_frame(0, frame), one_frame(1, frame))):
                image[2 + frame, row] = jnp.concatenate(sides, axis=-1).astype(BF16)
        for d in range(4):
            outs[d][...] = image[pl.ds(lax.rem(place + d, 4), 3)]
        return

    def add_up(video, carry):
        for frame in range(4):
            for row, summed in enumerate(one_frame(video, frame)):
                outs[0][video, frame, row] = summed.astype(BF16)
        return carry

    lax.fori_loop(0, 2, add_up, 0)


def run_middle(scalars, gain, held, parts, pieces, proj=None):
    last = proj is not None
    out_rows, columns, n = held.shape[2:]
    rows, source = parts[0].shape[2:4]
    total = 8 * rows * columns
    if last:
        out_shape = [jax.ShapeDtypeStruct((3, out_rows, columns, 2 * n), BF16)] * 4
    else:
        out_shape = [jax.ShapeDtypeStruct((2, 4, out_rows, columns, n), BF16)]
    operands = [scalars, gain, held] + parts + pieces + ([proj] if last else [])
    scratch = [
        pltpu.VMEM((4, 288, 9 * n), BF16),
        pltpu.VMEM((total, 1152), BF16),
        pltpu.VMEM((total, 9 * n), F32),
        pltpu.VMEM((total, n), F32),
    ]
    if last:
        scratch.append(pltpu.VMEM((6, out_rows, columns, 2 * n), BF16))
    return pl.pallas_call(
        functools.partial(middle_kernel, last, len(pieces)),
        out_shape=out_shape,
        in_specs=[SMEM] + [VMEM] * (len(operands) - 1),
        out_specs=[VMEM] * len(out_shape),
        scratch_shapes=scratch,
        compiler_params=PARAMS,
        cost_estimate=pl.CostEstimate(flops=8 * 10**9, bytes_accessed=4 * 2**20, transcendentals=0),
    )(*operands)


def last_held_kernel(scalar_ref, cache_ref, weight_ref, out_ref, stacked):
    columns, channels, n = 128, 192, 96
    place = scalar_ref[0]
    fine = spreader(columns, columns, False)
    out_ref[...] = jnp.zeros(out_ref.shape, F32)

    def one_video(video, carry):
        for frame in range(2):

            @pl.when(place + frame < 2)
            def _():
                for row in range(10):
                    values = cache_ref[video, jnp.minimum(place + frame, 1), row]
                    spread = dot(fine, values).astype(BF16)
                    for tap in range(3):
                        stacked[tap, row * columns : (row + 1) * columns, :] = spread[
                            tap * columns : (tap + 1) * columns
                        ]
                for row_tap in range(3):
                    part = None
                    for tap in range(3):
                        term = dot(
                            stacked[tap, row_tap * columns : (row_tap + 8) * columns, :],
                            weight_ref[frame, tap * channels : (tap + 1) * channels, n * row_tap : n * (row_tap + 1)],
                        )
                        part = term if part is None else part + term
                    out_ref[video] += part

        return carry

    lax.fori_loop(0, 2, one_video, 0)


def run_last_held(scalars, cache, weight):
    return pl.pallas_call(
        last_held_kernel,
        out_shape=jax.ShapeDtypeStruct((2, 1024, 96), F32),
        in_specs=[SMEM] + [VMEM] * 2,
        out_specs=VMEM,
        scratch_shapes=[pltpu.VMEM((3, 1280, 192), BF16)],
        compiler_params=PARAMS,
        cost_estimate=pl.CostEstimate(flops=8 * 10**9, bytes_accessed=4 * 2**20, transcendentals=0),
    )(scalars, cache, weight)


def last_kernel(scalar_ref, gain_ref, held_ref, weight_ref, proj_ref, *refs):
    parts, (out_ref, stacked, summed) = refs[:4], refs[4:]
    columns, channels, n = 128, 192, 96
    place = scalar_ref[0]
    coarse = spreader(columns, 64, True)
    middle = spreader(columns, 64, True, (1,))
    places = []
    for d in range(4):
        lane = 48 * lax.rem(place + 4 - d, 4)
        both = placer(96, 512, lane, 0, 48) + placer(96, 512, lane + 256, 48, 96)
        places.append(both.astype(BF16))

    for frame in (2, 1, 0):

        @pl.when(place + frame >= 2)
        def _():
            x = None
            for part, at in zip(parts, places):
                term = dot(part[frame].reshape(384, 96), at)
                x = term if x is None else x + term
            for video in range(2):
                own = x[:, 256 * video : 256 * video + channels]
                if frame == 2:
                    inputs = own.astype(BF16)
                    for row in range(4):
                        side = dot(middle, inputs[64 * (row + 1) : 64 * (row + 2)]).astype(BF16)
                        side = dot(side, proj_ref[...])
                        for copy in (2 * row, 2 * row + 1):
                            low = copy * columns
                            summed[video, low : low + columns, :] = side + held_ref[video, low : low + columns, :]
                active = normed(own, gain_ref[...])
                for row in range(6):
                    spread = dot(coarse, active[64 * row : 64 * (row + 1)]).astype(BF16)
                    for tap in range(3):
                        stacked[video, tap, row * columns : (row + 1) * columns, :] = spread[
                            tap * columns : (tap + 1) * columns
                        ]
            for video in range(2):
                product = None
                for tap in range(3):
                    term = dot(
                        stacked[video, tap],
                        weight_ref[frame, tap * channels : (tap + 1) * channels, :],
                    )
                    product = term if product is None else product + term
                for row in range(8):
                    part = None
                    for row_tap in range(3):
                        held_row = (row + row_tap + 1) // 2
                        term = product[
                            held_row * columns : (held_row + 1) * columns, n * row_tap : n * (row_tap + 1)
                        ]
                        part = term if part is None else part + term
                    summed[video, row * columns : (row + 1) * columns, :] += part

    for video in range(2):
        for row in range(8):
            out_ref[video, row] = summed[video, row * columns : (row + 1) * columns, :].T.astype(BF16)


def run_last(scalars, gain, held, weight, proj, parts):
    return pl.pallas_call(
        last_kernel,
        out_shape=jax.ShapeDtypeStruct((2, 8, 96, 128), BF16),
        in_specs=[SMEM] + [VMEM] * 8,
        out_specs=VMEM,
        scratch_shapes=[
            pltpu.VMEM((2, 3, 768, 192), BF16),
            pltpu.VMEM((2, 1024, 96), F32),
        ],
        compiler_params=PARAMS,
        cost_estimate=pl.CostEstimate(flops=10**10, bytes_accessed=4 * 2**20, transcendentals=0),
    )(scalars, gain, held, weight, proj, *parts)


def shards(
    features,
    cache_zero,
    cache_one,
    cache_two,
    cache_three,
    gain_zero,
    gain_one,
    gain_two,
    gain_three,
    weight_zero,
    weight_one,
    weight_two,
    weight_three,
    proj_two,
    proj_three,
):
    place = lax.axis_index("xlo") * 2 + lax.axis_index("core")
    row_at = lax.axis_index(ROWS)
    scalars = jnp.stack([place, lax.axis_index("y"), row_at == 0, row_at == 63, lax.axis_index("z")]).astype(jnp.int32)

    def quarter(x):
        width = x.shape[-1] // 4
        return lax.dynamic_slice_in_dim(x, place * width, width, x.ndim - 1)

    mixed = jnp.concatenate([quarter(weight_two).reshape(18, 432), weight_three.reshape(18, 432)], axis=1)
    first_two = [quarter(weight).reshape(18, 864) for weight in (weight_zero, weight_one)]
    shard = jnp.concatenate(first_two + [mixed, jnp.zeros((2, 864), BF16)], axis=0)
    plane, plane2 = run_plane(scalars, ring_z(with_other_plane(shard)))
    ring = share_ring(plane)
    pieces0, pieces1 = ring[:4], ring[:3] + ring[4:]
    start, swapped = with_halos(
        jnp.concatenate([cache_zero, features], axis=1),
        cache_one,
        cache_two,
        cache_three,
        plane,
        ring[1:3],
        ring[3:],
    )

    own0 = run_first(scalars, start, gain_zero[None], quarter(start[:, 2:, 1:4]), pieces0)
    parts1 = share_segment([own0] * 4)
    held_one, held_two, held_three = later_halos(swapped, cache_one, cache_two, cache_three, own0)
    pieces2 = share_column(after(plane2, own0))
    before1 = run_held(scalars, held_one, pieces1, 4, 96)
    own1 = run_middle(scalars, gain_one[None], before1, parts1, pieces1)[0]
    parts2 = share_segment([own1] * 4)
    before2 = run_held(scalars, held_two, pieces2, 6, 48)
    sent = run_middle(scalars, gain_two[None], before2, parts2, pieces2, quarter(proj_two))
    parts3 = share_segment(sent)

    w3 = run_halves(scalars, pieces2)
    before3 = run_last_held(scalars, held_three, w3)
    out = run_last(scalars, gain_three[None], before3, w3, proj_three, parts3)
    return out.transpose(0, 2, 1, 3)[:, None]


def solution(mesh):
    fine_mesh = Mesh(mesh.devices.reshape(2, 2, 4, 2, 8), ALL)
    slab = P(None, None, ROWS, None, None)
    shard = P(ROWS, None, None, None)
    return jax.shard_map(
        shards,
        mesh=fine_mesh,
        in_specs=(slab,) * 5 + (P(),) * 4 + (shard,) * 4 + (P(),) * 2,
        out_specs=P(None, SEG, None, ROWS, None),
        check_vma=False,
    )
```

```python
import functools

import jax
import jax.numpy as jnp
from jax import lax
from jax.experimental import pallas as pl
from jax.experimental.pallas import tpu as pltpu
from jax.sharding import Mesh
from jax.sharding import PartitionSpec as P

EPSILON = 1e-06
ROWS = ("y", "xhi", "z")
SEG = ("xlo", "core")
ALL = SEG + ROWS
BF16 = jnp.bfloat16
F32 = jnp.float32


def after(x, *others):
    return lax.optimization_barrier((x,) + others)[0]


def fetch_rows(x, by):
    pairs = []
    for segment in range(4):
        step = by if segment % 2 == 0 else -by
        pairs += [(segment * 64 + r + step, segment * 64 + r) for r in range(64) if 0 <= r + step < 64]
    return lax.ppermute(x, ALL, pairs)


def both_sides(own):
    core = lax.axis_index("core")
    other = lax.ppermute(own, "core", [(0, 1), (1, 0)])
    return jnp.where(core == 1, own, other), jnp.where(core == 0, own, other)


def with_halos(start, one, two, three, first_after, second_after, swap_after):
    upper = lax.axis_index("core")
    two_rows = lax.dynamic_slice_in_dim(two, upper * (two.shape[2] - 2), 2, 2)
    three_rows = lax.dynamic_slice_in_dim(three, upper * (three.shape[2] - 1), 1, 2)[:, :, 0]
    sides = jnp.concatenate([three_rows[:, 0], three_rows[:, 1]], axis=-1)
    first = after(start.reshape(-1, 384), first_after)
    second = jnp.concatenate([x.reshape(-1, 384) for x in (one, two_rows, sides)], axis=0)
    got = fetch_rows(first, 1), fetch_rows(first, 2), fetch_rows(after(second, *second_after), 1)
    got = lax.optimization_barrier(got + tuple(swap_after))[:3]
    rims = both_sides(jnp.concatenate(got, axis=0))
    nears = [rim[:192].reshape(start.shape) for rim in rims]
    fars = [rim[192:384].reshape(start.shape) for rim in rims]
    ones = [rim[384:640].reshape(2, 2, 2, 32, 384) for rim in rims]
    twos = [rim[640:1152].reshape(2, 2, 2, 64, 384) for rim in rims]
    sides = [rim[1152:].reshape(2, 128, 384) for rim in rims]
    threes = [jnp.stack([x[..., :192], x[..., 192:]], axis=1)[:, :, None] for x in sides]
    return (
        jnp.concatenate([fars[0], nears[0], start, nears[1], fars[1]], axis=2),
        jnp.concatenate([ones[0], one, ones[1]], axis=2),
        jnp.concatenate([twos[0], two, twos[1]], axis=2),
        threes,
    )


def with_other_plane(x):
    other = lax.ppermute(x, "xhi", [(0, 1), (1, 0)])
    first = lax.axis_index("xhi") == 0
    return jnp.concatenate([jnp.where(first, x, other), jnp.where(first, other, x)], axis=0)


def ring_z(mine):
    up = [(i, (i + 1) % 8) for i in range(8)]
    down = [(j, i) for i, j in up]
    half = mine.shape[0] // 2
    pieces = [mine]
    rising = falling = mine
    for step in range(1, 5):
        if step == 4:
            rising, falling = rising[:half], falling[half:]
        rising = lax.ppermute(rising, "z", up)
        falling = lax.ppermute(falling, "z", down)
        pieces += [rising, falling]
    return pieces


def share_ring(block, *wait_for):
    up = [(i, (i + 1) % 4) for i in range(4)]
    down = [(j, i) for i, j in up]
    half = block.shape[0] // 2
    sent = after(block, *wait_for) if wait_for else block
    from_below = lax.ppermute(sent, "y", up)
    from_above = lax.ppermute(sent, "y", down)
    far_top = lax.ppermute(from_below[:half], "y", up)
    far_bottom = lax.ppermute(from_above[half:], "y", down)
    return [block, from_below, from_above, far_top, far_bottom]


def share_column(block):
    return [block] + [
        lax.ppermute(block, "y", [(i, (i + d) % 4) for i in range(4)]) for d in (1, 3, 2)
    ]


def share_segment(pieces):
    return [pieces[0]] + [
        lax.ppermute(pieces[d], SEG, [(i, (i + d) % 4) for i in range(4)]) for d in (1, 2, 3)
    ]


VMEM = pl.BlockSpec(memory_space=pltpu.VMEM)
SMEM = pl.BlockSpec(memory_space=pltpu.SMEM)
PARAMS = pltpu.CompilerParams(vmem_limit_bytes=44 * 2**20)


def spreader(columns, source, doubled, taps=(0, 1, 2)):
    parts = []
    for tap in taps:
        at = lax.broadcasted_iota(jnp.int32, (columns, source), 0) + (tap - 1)
        held = lax.broadcasted_iota(jnp.int32, (columns, source), 1)
        low = 2 * held if doubled else held
        high = low + 1 if doubled else low
        parts.append(jnp.where((at >= low) & (at <= high), 1.0, 0.0).astype(BF16))
    return parts[0] if len(parts) == 1 else jnp.concatenate(parts, axis=0)


def block_spreader(rows, columns, source, doubled, taps=(0, 1, 2)):
    shape = (rows * columns, rows * source)
    out = lax.broadcasted_iota(jnp.int32, shape, 0)
    held = lax.broadcasted_iota(jnp.int32, shape, 1)
    bits, held_bits = columns.bit_length() - 1, source.bit_length() - 1
    same = (out >> bits) == (held >> held_bits)
    low = held & (source - 1)
    low = 2 * low if doubled else low
    high = low + 1 if doubled else low
    parts = []
    for tap in taps:
        at = (out & (columns - 1)) + (tap - 1)
        parts.append(jnp.where(same & (at >= low) & (at <= high), 1.0, 0.0).astype(BF16))
    return parts[0] if len(parts) == 1 else jnp.concatenate(parts, axis=0)


def placer(width, lanes, offset, low=0, high=None):
    row = lax.broadcasted_iota(jnp.int32, (width, lanes), 0)
    lane = lax.broadcasted_iota(jnp.int32, (width, lanes), 1)
    hit = (lane == row - low + offset) & (row >= low) & (row < (width if high is None else high))
    return jnp.where(hit, 1.0, 0.0)


def normed(x, gain):
    scaled = x * lax.rsqrt(jnp.mean(x * x, axis=-1, keepdims=True) + EPSILON)
    scaled = scaled * gain
    return (scaled / (1.0 + jnp.exp(-scaled))).astype(BF16)


def set_weights(at, pieces, whole, base=0):
    for piece, off in zip(pieces, (0, 3, 1, 2)):
        low = 0 if off == 2 else base
        whole[lax.rem(at + off, 4)] = piece[low : low + 288]


def set_last_weights(at, pieces, whole, lane):
    lanes = pl.ds(lane, whole.shape[2])
    for piece, off in zip(pieces, (0, 3, 1, 2)):
        whole[lax.rem(at + off, 4)] = piece[:, lanes]


def put_taps(stacked, row_at, columns, spread):
    channels = spread.shape[1]
    for tap in range(3):
        stacked[pl.ds(row_at, columns), tap * channels : (tap + 1) * channels] = spread[
            tap * columns : (tap + 1) * columns
        ]


def multiply_all(stacked, whole, product, total):
    chunk = next(c for c in (512, 480, 384, 320, 256, 192, 128, 96, 64) if total % c == 0)

    def multiply(step, carry):
        at = pl.multiple_of(step * chunk, chunk)
        weight = whole[...].reshape(4 * whole.shape[1], whole.shape[2])
        product[pl.ds(at, chunk), :] = jnp.dot(
            stacked[pl.ds(at, chunk), :], weight, preferred_element_type=F32
        )
        return carry

    lax.fori_loop(0, total // chunk, multiply, 0)


def dot(a, b):
    return jnp.dot(a, b, preferred_element_type=F32)


def plane_kernel(scalar_ref, *refs):
    pieces, outs, held = refs[:9], refs[9:11], refs[11]
    at = scalar_ref[4]
    for piece, off in zip(pieces[:7], (0, 7, 1, 6, 2, 5, 3)):
        held[lax.rem(at + off, 8)] = piece[...]
    held[lax.rem(at + 4, 8), :56] = pieces[7][...]
    held[lax.rem(at + 4, 8), 56:] = pieces[8][...]
    for matrix, (out, base) in enumerate(((outs[0], 0), (outs[0], 288), (outs[1], 0))):
        for block in range(16):
            low = 56 * (block // 8) + 18 * matrix
            out[base + 18 * block : base + 18 * (block + 1), :] = held[block % 8, low : low + 18, :]


def run_plane(scalars, pieces):
    return pl.pallas_call(
        plane_kernel,
        out_shape=[jax.ShapeDtypeStruct((576, 864), BF16), jax.ShapeDtypeStruct((288, 864), BF16)],
        in_specs=[SMEM] + [VMEM] * 9,
        out_specs=[VMEM] * 2,
        scratch_shapes=[pltpu.VMEM((8, 112, 864), BF16)],
        compiler_params=PARAMS,
        cost_estimate=pl.CostEstimate(flops=10**8, bytes_accessed=4 * 2**20, transcendentals=0),
    )(scalars, *pieces)


def halves_kernel(scalar_ref, *refs):
    pieces, (out_ref, whole) = refs[:4], refs[4:]
    set_last_weights(scalar_ref[1], pieces, whole, 432)
    row = lax.broadcasted_iota(jnp.int32, (72, 144), 0)
    lane = lax.broadcasted_iota(jnp.int32, (72, 144), 1)
    picks = [jnp.where(lane == 2 * row + half, 1.0, 0.0).astype(BF16) for half in range(2)]
    for block in range(8):
        rows = whole[block // 2, 144 * (block % 2) : 144 * (block % 2 + 1), :]
        full = jnp.concatenate([dot(pick, rows) for pick in picks], axis=-1)
        for tap in range(3):
            out_ref[tap, 72 * block : 72 * (block + 1), :] = full[:, 288 * tap : 288 * (tap + 1)].astype(BF16)


def run_halves(scalars, pieces):
    return pl.pallas_call(
        halves_kernel,
        out_shape=jax.ShapeDtypeStruct((3, 576, 288), BF16),
        in_specs=[SMEM] + [VMEM] * 4,
        out_specs=VMEM,
        scratch_shapes=[pltpu.VMEM((4, 288, 432), BF16)],
        compiler_params=PARAMS,
        cost_estimate=pl.CostEstimate(flops=10**8, bytes_accessed=4 * 2**20, transcendentals=0),
    )(scalars, *pieces)


def held_kernel(scalar_ref, cache_ref, *refs):
    pieces, (out_ref, whole, stacked, product) = refs[:-4], refs[-4:]
    rows, columns = cache_ref.shape[2], cache_ref.shape[3]
    out_rows, n = out_ref.shape[2], out_ref.shape[4]
    if n == 96:
        set_weights(scalar_ref[1], pieces, whole, 288)
    else:
        set_last_weights(scalar_ref[1], pieces, whole, 0)
    fine = spreader(columns, columns, False)
    size = rows * columns

    def fill(frame, carry):
        for row in range(rows):
            at = pl.multiple_of(frame * size + row * columns, columns)
            values = cache_ref[frame // 2, lax.rem(frame, 2), row]
            put_taps(stacked, at, columns, dot(fine, values).astype(BF16))
        return carry

    lax.fori_loop(0, 4, fill, 0)
    multiply_all(stacked, whole, product, 4 * size)

    def add_up(video, carry):
        for frame in range(2):
            for row in range(out_rows):
                summed = None
                for frame_tap in range(2 - frame):
                    for row_tap in range(3):
                        at = (frame + frame_tap) * size + (row + row_tap) * columns
                        at = pl.multiple_of(video * 2 * size + at, columns)
                        lane = (3 * frame_tap + row_tap) * n
                        part = product[pl.ds(at, columns), lane : lane + n]
                        summed = part if summed is None else summed + part
                out_ref[video, frame, row] = summed
        return carry

    lax.fori_loop(0, 2, add_up, 0)


def run_held(scalars, cache, pieces, out_rows, n):
    rows, columns, channels = cache.shape[2:]
    total = 4 * rows * columns
    return pl.pallas_call(
        held_kernel,
        out_shape=jax.ShapeDtypeStruct((2, 2, out_rows, columns, n), F32),
        in_specs=[SMEM] + [VMEM] * (1 + len(pieces)),
        out_specs=VMEM,
        scratch_shapes=[
            pltpu.VMEM((4, 3 * channels // 4, 9 * n), BF16),
            pltpu.VMEM((total, 3 * channels), BF16),
            pltpu.VMEM((total, 9 * n), F32),
        ],
        compiler_params=PARAMS,
        cost_estimate=pl.CostEstimate(flops=6 * 10**9, bytes_accessed=4 * 2**20, transcendentals=0),
    )(scalars, cache, *pieces)


def first_kernel(scalar_ref, x_ref, gain_ref, own_ref, *refs):
    pieces, (out_ref, whole, stacked, product) = refs[:-4], refs[-4:]
    set_weights(scalar_ref[1], pieces, whole)
    columns, rows, out_rows, n = 16, 5, 3, 96
    size = rows * columns
    fine = block_spreader(8, columns, columns, False)

    def fill(video, carry):
        for frame in range(6):
            u = x_ref[video, frame].reshape(size, 384)
            if frame >= 2:
                u = normed(u.astype(F32), gain_ref[...])
            at = pl.multiple_of((video * 6 + frame) * size, size)
            for tap in range(3):
                part = fine[128 * tap : 128 * tap + size, :size]
                stacked[pl.ds(at, size), 384 * tap : 384 * (tap + 1)] = dot(part, u).astype(BF16)
        return carry

    lax.fori_loop(0, 2, fill, 0)
    multiply_all(stacked, whole, product, 12 * size)

    def add_up(video, carry):
        for frame in range(4):
            for row in range(out_rows):
                summed = own_ref[video, frame, row].astype(F32)
                for frame_tap in range(3):
                    for row_tap in range(3):
                        at = (video * 6 + frame + frame_tap) * size + (row + row_tap) * columns
                        lane = (3 * frame_tap + row_tap) * n
                        summed = summed + product[pl.ds(pl.multiple_of(at, columns), columns), lane : lane + n]
                if row == 0:
                    summed = jnp.where(scalar_ref[2] == 1, 0.0, summed)
                if row == out_rows - 1:
                    summed = jnp.where(scalar_ref[3] == 1, 0.0, summed)
                out_ref[video, frame, row] = summed.astype(BF16)
        return carry

    lax.fori_loop(0, 2, add_up, 0)


def run_first(scalars, x, gain, own, pieces):
    total = 12 * 5 * 16
    return pl.pallas_call(
        first_kernel,
        out_shape=jax.ShapeDtypeStruct((2, 4, 3, 16, 96), BF16),
        in_specs=[SMEM] + [VMEM] * 7,
        out_specs=VMEM,
        scratch_shapes=[
            pltpu.VMEM((4, 288, 864), BF16),
            pltpu.VMEM((total, 1152), BF16),
            pltpu.VMEM((total, 864), F32),
        ],
        compiler_params=PARAMS,
        cost_estimate=pl.CostEstimate(flops=3 * 10**9, bytes_accessed=4 * 2**20, transcendentals=0),
    )(scalars, x, gain, own, *pieces)


def middle_kernel(last, n_pieces, scalar_ref, gain_ref, held_ref, *refs):
    parts, pieces, refs = refs[:4], refs[4 : 4 + n_pieces], refs[4 + n_pieces :]
    if last:
        proj_ref, outs, refs = refs[0], refs[1:5], refs[5:]
    else:
        outs, refs = refs[:1], refs[1:]
    whole, stacked, product, shortcut = refs[:4]
    place = scalar_ref[0]
    if last:
        set_last_weights(scalar_ref[1], pieces, whole, 0)
    else:
        set_weights(scalar_ref[1], pieces, whole, 288)
    rows, source = parts[0].shape[2], parts[0].shape[3]
    out_rows, columns, n = held_ref.shape[2], held_ref.shape[3], held_ref.shape[4]
    coarse = block_spreader(rows, columns, source, True)
    middle = block_spreader(rows, columns, source, True, (1,))
    frame_size, u_size = rows * source, rows * columns
    places = [placer(96, 384, 96 * lax.rem(place + 4 - d, 4)).astype(BF16) for d in range(4)]

    def fill(step, carry):
        video, frame = step // 4, lax.rem(step, 4)
        x = None
        for part, at in zip(parts, places):
            term = dot(part[video, frame].reshape(frame_size, 96), at)
            x = term if x is None else x + term
        spread = dot(coarse, normed(x, gain_ref[...])).astype(BF16)
        at = pl.ds(pl.multiple_of(step * u_size, u_size), u_size)
        for tap in range(3):
            stacked[at, tap * 384 : (tap + 1) * 384] = spread[tap * u_size : (tap + 1) * u_size]
        if last:
            own = dot(dot(middle, x.astype(BF16)).astype(BF16), proj_ref[...])
        else:
            own = dot(middle, parts[0][video, frame].reshape(frame_size, 96))
        shortcut[at, :] = own
        return carry

    lax.fori_loop(0, 8, fill, 0, unroll=2)
    multiply_all(stacked, whole, product, 8 * u_size)

    def one_frame(video, frame):
        sums = []
        for row in range(rows):
            for row_tap in range(3):
                summed = None
                for frame_tap in range(max(0, 2 - frame), 3):
                    at = (video * 4 + frame + frame_tap - 2) * u_size + row * columns
                    lane = (3 * frame_tap + row_tap) * n
                    part = product[pl.ds(pl.multiple_of(at, columns), columns), lane : lane + n]
                    summed = part if summed is None else summed + part
                sums.append(summed)
        outcomes = []
        for row in range(out_rows):
            at = (video * 4 + frame) * u_size + (row + 1) // 2 * columns
            summed = shortcut[pl.ds(pl.multiple_of(at, columns), columns), :]
            for row_tap in range(3):
                summed = summed + sums[3 * ((row + row_tap) // 2) + row_tap]
            if frame < 2:
                summed = summed + held_ref[video, frame, row]
            if row == 0:
                summed = jnp.where(scalar_ref[2] == 1, 0.0, summed)
            if row == out_rows - 1:
                summed = jnp.where(scalar_ref[3] == 1, 0.0, summed)
            outcomes.append(summed)
        return outcomes

    if last:
        image = refs[4]
        image[0] = jnp.zeros(image.shape[1:], BF16)
        image[1] = jnp.zeros(image.shape[1:], BF16)
        for frame in range(4):
            for row, sides in enumerate(zip(one_frame(0, frame), one_frame(1, frame))):
                image[2 + frame, row] = jnp.concatenate(sides, axis=-1).astype(BF16)
        for d in range(4):
            outs[d][...] = image[pl.ds(lax.rem(place + d, 4), 3)]
        return

    def add_up(video, carry):
        for frame in range(4):
            for row, summed in enumerate(one_frame(video, frame)):
                outs[0][video, frame, row] = summed.astype(BF16)
        return carry

    lax.fori_loop(0, 2, add_up, 0)


def run_middle(scalars, gain, held, parts, pieces, proj=None):
    last = proj is not None
    out_rows, columns, n = held.shape[2:]
    rows, source = parts[0].shape[2:4]
    total = 8 * rows * columns
    if last:
        out_shape = [jax.ShapeDtypeStruct((3, out_rows, columns, 2 * n), BF16)] * 4
    else:
        out_shape = [jax.ShapeDtypeStruct((2, 4, out_rows, columns, n), BF16)]
    operands = [scalars, gain, held] + parts + pieces + ([proj] if last else [])
    scratch = [
        pltpu.VMEM((4, 288, 9 * n), BF16),
        pltpu.VMEM((total, 1152), BF16),
        pltpu.VMEM((total, 9 * n), F32),
        pltpu.VMEM((total, n), F32),
    ]
    if last:
        scratch.append(pltpu.VMEM((6, out_rows, columns, 2 * n), BF16))
    return pl.pallas_call(
        functools.partial(middle_kernel, last, len(pieces)),
        out_shape=out_shape,
        in_specs=[SMEM] + [VMEM] * (len(operands) - 1),
        out_specs=[VMEM] * len(out_shape),
        scratch_shapes=scratch,
        compiler_params=PARAMS,
        cost_estimate=pl.CostEstimate(flops=8 * 10**9, bytes_accessed=4 * 2**20, transcendentals=0),
    )(*operands)


def last_held_kernel(scalar_ref, cache_ref, weight_ref, out_ref, stacked):
    columns, channels, n = 128, 192, 96
    place = scalar_ref[0]
    fine = spreader(columns, columns, False)
    out_ref[...] = jnp.zeros(out_ref.shape, F32)

    def one_video(video, carry):
        for frame in range(2):

            @pl.when(place + frame < 2)
            def _():
                for row in range(10):
                    values = cache_ref[video, jnp.minimum(place + frame, 1), row]
                    spread = dot(fine, values).astype(BF16)
                    for tap in range(3):
                        stacked[tap, row * columns : (row + 1) * columns, :] = spread[
                            tap * columns : (tap + 1) * columns
                        ]
                for row_tap in range(3):
                    part = None
                    for tap in range(3):
                        term = dot(
                            stacked[tap, row_tap * columns : (row_tap + 8) * columns, :],
                            weight_ref[frame, tap * channels : (tap + 1) * channels, n * row_tap : n * (row_tap + 1)],
                        )
                        part = term if part is None else part + term
                    out_ref[video] += part

        return carry

    lax.fori_loop(0, 2, one_video, 0)


def run_last_held(scalars, cache, weight):
    return pl.pallas_call(
        last_held_kernel,
        out_shape=jax.ShapeDtypeStruct((2, 1024, 96), F32),
        in_specs=[SMEM] + [VMEM] * 2,
        out_specs=VMEM,
        scratch_shapes=[pltpu.VMEM((3, 1280, 192), BF16)],
        compiler_params=PARAMS,
        cost_estimate=pl.CostEstimate(flops=8 * 10**9, bytes_accessed=4 * 2**20, transcendentals=0),
    )(scalars, cache, weight)


def last_kernel(scalar_ref, gain_ref, held_ref, weight_ref, proj_ref, *refs):
    parts, (out_ref, stacked, summed) = refs[:4], refs[4:]
    columns, channels, n = 128, 192, 96
    place = scalar_ref[0]
    coarse = spreader(columns, 64, True)
    middle = spreader(columns, 64, True, (1,))
    places = []
    for d in range(4):
        lane = 48 * lax.rem(place + 4 - d, 4)
        both = placer(96, 512, lane, 0, 48) + placer(96, 512, lane + 256, 48, 96)
        places.append(both.astype(BF16))

    for frame in (2, 1, 0):

        @pl.when(place + frame >= 2)
        def _():
            x = None
            for part, at in zip(parts, places):
                term = dot(part[frame].reshape(384, 96), at)
                x = term if x is None else x + term
            for video in range(2):
                own = x[:, 256 * video : 256 * video + channels]
                if frame == 2:
                    inputs = own.astype(BF16)
                    for row in range(4):
                        side = dot(middle, inputs[64 * (row + 1) : 64 * (row + 2)]).astype(BF16)
                        side = dot(side, proj_ref[...])
                        for copy in (2 * row, 2 * row + 1):
                            low = copy * columns
                            summed[video, low : low + columns, :] = side + held_ref[video, low : low + columns, :]
                active = normed(own, gain_ref[...])
                for row in range(6):
                    spread = dot(coarse, active[64 * row : 64 * (row + 1)]).astype(BF16)
                    for tap in range(3):
                        stacked[video, tap, row * columns : (row + 1) * columns, :] = spread[
                            tap * columns : (tap + 1) * columns
                        ]
            for video in range(2):
                product = None
                for tap in range(3):
                    term = dot(
                        stacked[video, tap],
                        weight_ref[frame, tap * channels : (tap + 1) * channels, :],
                    )
                    product = term if product is None else product + term
                for row in range(8):
                    part = None
                    for row_tap in range(3):
                        held_row = (row + row_tap + 1) // 2
                        term = product[
                            held_row * columns : (held_row + 1) * columns, n * row_tap : n * (row_tap + 1)
                        ]
                        part = term if part is None else part + term
                    summed[video, row * columns : (row + 1) * columns, :] += part

    for video in range(2):
        for row in range(8):
            out_ref[video, row] = summed[video, row * columns : (row + 1) * columns, :].T.astype(BF16)


def run_last(scalars, gain, held, weight, proj, parts):
    return pl.pallas_call(
        last_kernel,
        out_shape=jax.ShapeDtypeStruct((2, 8, 96, 128), BF16),
        in_specs=[SMEM] + [VMEM] * 8,
        out_specs=VMEM,
        scratch_shapes=[
            pltpu.VMEM((2, 3, 768, 192), BF16),
            pltpu.VMEM((2, 1024, 96), F32),
        ],
        compiler_params=PARAMS,
        cost_estimate=pl.CostEstimate(flops=10**10, bytes_accessed=4 * 2**20, transcendentals=0),
    )(scalars, gain, held, weight, proj, *parts)


def shards(
    features,
    cache_zero,
    cache_one,
    cache_two,
    cache_three,
    gain_zero,
    gain_one,
    gain_two,
    gain_three,
    weight_zero,
    weight_one,
    weight_two,
    weight_three,
    proj_two,
    proj_three,
):
    place = lax.axis_index("xlo") * 2 + lax.axis_index("core")
    row_at = lax.axis_index(ROWS)
    scalars = jnp.stack([place, lax.axis_index("y"), row_at == 0, row_at == 63, lax.axis_index("z")]).astype(jnp.int32)

    def quarter(x):
        width = x.shape[-1] // 4
        return lax.dynamic_slice_in_dim(x, place * width, width, x.ndim - 1)

    mixed = jnp.concatenate([quarter(weight_two).reshape(18, 432), weight_three.reshape(18, 432)], axis=1)
    first_two = [quarter(weight).reshape(18, 864) for weight in (weight_zero, weight_one)]
    shard = jnp.concatenate(first_two + [mixed, jnp.zeros((2, 864), BF16)], axis=0)
    plane, plane2 = run_plane(scalars, ring_z(with_other_plane(shard)))
    ring = share_ring(plane)
    pieces0, pieces1 = ring[:4], ring[:3] + ring[4:]
    start, held_one, held_two, rim_three = with_halos(
        jnp.concatenate([cache_zero, features], axis=1),
        cache_one,
        cache_two,
        cache_three,
        plane,
        ring[1:3],
        ring[3:],
    )

    own0 = run_first(scalars, start, gain_zero[None], quarter(start[:, 2:, 1:4]), pieces0)
    parts1 = share_segment([own0] * 4)
    pieces2 = share_column(after(plane2, own0))
    before1 = run_held(scalars, held_one, pieces1, 4, 96)
    own1 = run_middle(scalars, gain_one[None], before1, parts1, pieces1)[0]
    parts2 = share_segment([own1] * 4)
    cache_three = after(cache_three, own1)
    held_three = jnp.concatenate([rim_three[0], cache_three, rim_three[1]], axis=2)
    before2 = run_held(scalars, held_two, pieces2, 6, 48)
    sent = run_middle(scalars, gain_two[None], before2, parts2, pieces2, quarter(proj_two))
    parts3 = share_segment(sent)

    w3 = run_halves(scalars, pieces2)
    before3 = run_last_held(scalars, held_three, w3)
    out = run_last(scalars, gain_three[None], before3, w3, proj_three, parts3)
    return out.transpose(0, 2, 1, 3)[:, None]


def solution(mesh):
    fine_mesh = Mesh(mesh.devices.reshape(2, 2, 4, 2, 8), ALL)
    slab = P(None, None, ROWS, None, None)
    shard = P(ROWS, None, None, None)
    return jax.shard_map(
        shards,
        mesh=fine_mesh,
        in_specs=(slab,) * 5 + (P(),) * 4 + (shard,) * 4 + (P(),) * 2,
        out_specs=P(None, SEG, None, ROWS, None),
        check_vma=False,
    )
```
